128 devices in a mesh: energy: 32 (over z, y, core), section: 4 (over x).
Axes of the slice: x: 4, y: 4, z: 4, core: 2. Of those that a mesh axis runs over, the one named last changes fastest.
Arguments:
- onsite: float32 [8, 256], P('section'), may hold values from -1 to 1
- hopping: float32 [8, 256, 256], P('section'), may hold values from -0.125 to 0.125
- coupling: float32 [8, 256, 256], P('section'), may hold values from -4 to 4
- broadening: float32 [32], P('energy'), may hold values from 1.5 to 3
- born_sigma: float32 [32, 8, 2, 256, 256], P('energy', 'section'), may hold values from -0.046875 to 0.046875
- phonon_shift: int32 [4], replicated, may hold values from -2 to 2
- phonon_local: float32 [4, 256, 256], replicated, may hold values from 0.5 to 4
- phonon_side: float32 [4, 256, 256], replicated, may hold values from 0.2 to 2
Outputs:
- next_sigma: float32 [32, 8, 2, 256, 256], P('energy', 'section')
The draws below stay inside these ranges and needn't reach their ends.
All inputs are finite; a program needn't handle non-finite values.
Results may differ from the reference program's by a relative error of at most 0.0001.
Values sent between devices are 32-bit elements; how exact they have to be, the bound alone decides.
A program may use at most 128 MiB of HBM per device.

```python
import math
import jax
import jax.numpy as jnp
from jax import lax

B = 256
MODES = 4
NS_ITERS = 3
OMAX = 2
NE = 32
NB = 8


def draw_coupling(key, part):
    base = jax.random.fold_in(key, 7)
    key_sign, key_size, key_dense = jax.random.split(base, 3)
    magnitude = jax.random.uniform(key_size, (NB, B), jnp.float32, 2.5, 3.5)
    spread = 1.0 / math.sqrt(8.0 * B)
    dense = jax.random.truncated_normal(key_dense, -6.0, 6.0, (NB, B, B), jnp.float32) * spread
    flips = jax.random.bernoulli(key_sign, 0.5, (NB, B))
    signed = jnp.where(flips, 1.0, -1.0).astype(jnp.float32) * magnitude
    diagonal = signed[:, :, None] * jnp.eye(B, dtype=jnp.float32)[None]
    return (diagonal + dense).astype(jnp.float32)


def place_ends(entries, key, low, top_value):
    longest = entries.shape.index(max(entries.shape))
    spots = []
    for shift in (0, 1):
        where = [jax.random.randint(jax.random.fold_in(key, axis), (), 0, length) for axis, length in enumerate(entries.shape)]
        where[longest] = (where[longest] + shift) % entries.shape[longest]
        spots.append(tuple(where))
    return entries.at[spots[0]].set(low).at[spots[1]].set(top_value)


def block_levels(key, extent, cuts, smallest, top_value):
    def one(dim, shards_of):
        steps = jax.random.uniform(jax.random.fold_in(jax.random.fold_in(key, 6), dim), (shards_of,), jnp.float32, smallest / len(cuts), top_value / len(cuts))
        return jnp.repeat(jnp.exp(steps), extent[dim] // shards_of).reshape((-1,) + (1,) * (len(extent) - dim - 1))

    gain = one(*cuts[0])
    for cut in cuts[1:]:
        gain = gain * one(*cut)
    return gain


def centred(rng, dims, scale, most, pieces=(), held_as=jnp.bfloat16):
    level = block_levels(rng, dims, pieces, -0.22, 0.18) if pieces else 1.0
    values = jax.random.normal(rng, dims, jnp.float32) * scale * level
    return jnp.minimum(jnp.maximum(values, -most), most).astype(held_as)


def setup_inputs(seed: int = 0) -> dict:
    streams_of = jax.random.split(jax.random.key(seed), 9)
    onsite = jnp.clip(jax.random.uniform(streams_of[0], (NB, B), jnp.float32, -1.0, 1.0) * block_levels(streams_of[0], (NB, B), ((0, 4),), -0.4, 0.0), -1.0, 1.0)
    hopping = centred(streams_of[1], (NB, B, B), (8 * B) ** -0.5, 0.125, ((0, 4),), jnp.float32)
    coupling = draw_coupling(jax.random.fold_in(streams_of[8], 71), 0)
    broadening = jnp.clip(jnp.exp(math.log(3.0) - 0.6931472 * jax.random.uniform(streams_of[3], (NE,), jnp.float32) ** block_levels(streams_of[3], (NE,), ((0, 32),), -0.2, 0.2)), 1.5, 3.0)
    born_sigma = centred(streams_of[4], (NE, NB, 2, B, B), (64 * B) ** -0.5, 0.046875, ((0, 32), (1, 4)), jnp.float32)
    phonon_shift = place_ends(jax.random.randint(streams_of[5], (MODES,), -OMAX, OMAX + 1), jax.random.fold_in(streams_of[5], 1), -OMAX, OMAX).astype(jnp.int32)
    phonon_local = jnp.clip(jnp.exp(jax.random.uniform(streams_of[6], (MODES, B, B), jnp.float32, math.log(0.5), math.log(4.0))), 0.5, 4.0)
    phonon_side = jnp.clip(jnp.exp(jax.random.uniform(streams_of[7], (MODES, B, B), jnp.float32, math.log(0.2), math.log(2.0))), 0.2, 2.0)
    return {"onsite": onsite, "hopping": hopping, "coupling": coupling, "broadening": broadening, "born_sigma": born_sigma, "phonon_shift": phonon_shift, "phonon_local": phonon_local, "phonon_side": phonon_side}


HIGH = lax.Precision.HIGHEST


def matmul(left, right):
    return jnp.matmul(left, right, precision=HIGH)


def complex_product(left, right):
    left_real = left[..., 0, :, :]
    left_imag = left[..., 1, :, :]
    right_real = right[..., 0, :, :]
    right_imag = right[..., 1, :, :]
    return jnp.stack([matmul(left_real, right_real) - matmul(left_imag, right_imag),
                      matmul(left_real, right_imag) + matmul(left_imag, right_real)], axis=-3)


def newton_inverse(matrix):
    dimension = matrix.shape[-1]
    identity = jnp.eye(dimension, dtype=jnp.float32)
    mat_real = matrix[..., 0, :, :]
    mat_imag = matrix[..., 1, :, :]
    diag_real = jnp.diagonal(mat_real, axis1=-2, axis2=-1)
    diag_imag = jnp.diagonal(mat_imag, axis1=-2, axis2=-1)
    modulus = diag_real * diag_real + diag_imag * diag_imag
    inv_real = diag_real / modulus
    inv_imag = -diag_imag / modulus
    col_real = inv_real[..., None, :]
    col_imag = inv_imag[..., None, :]
    scaled_real = mat_real * col_real - mat_imag * col_imag
    scaled_imag = mat_real * col_imag + mat_imag * col_real
    remain_real = 2.0 * identity - scaled_real
    remain_imag = -scaled_imag
    row_real = inv_real[..., :, None]
    row_imag = inv_imag[..., :, None]
    current = jnp.stack([row_real * remain_real - row_imag * remain_imag,
                         row_real * remain_imag + row_imag * remain_real], axis=-3)
    for repeat in range(NS_ITERS - 1):
        product = complex_product(matrix, current)
        remainder = jnp.stack([2.0 * identity - product[..., 0, :, :], -product[..., 1, :, :]], axis=-3)
        current = complex_product(current, remainder)
    return current


def left_couple(link, green_block):
    transposed = jnp.swapaxes(link, -1, -2)[..., None, :, :]
    return matmul(matmul(transposed, green_block), link[..., None, :, :])


def right_couple(link, green_block):
    transposed = jnp.swapaxes(link, -1, -2)[..., None, :, :]
    return matmul(matmul(link[..., None, :, :], green_block), transposed)


def reference(onsite, hopping, coupling, broadening, born_sigma, phonon_shift, phonon_local, phonon_side):
    dimension = onsite.shape[1]
    block_count = onsite.shape[0]
    identity = jnp.eye(dimension, dtype=jnp.float32)
    hamiltonian = 0.5 * (hopping + jnp.swapaxes(hopping, -1, -2)) + onsite[:, :, None] * identity
    energy_values = -2.0 + 4.0 * jnp.arange(NE, dtype=jnp.float32) / (NE - 1)
    sys_real = energy_values[:, None, None, None] * identity - hamiltonian[None] - born_sigma[:, :, 0]
    sys_imag = broadening[:, None, None, None] * identity - born_sigma[:, :, 1]
    system = jnp.stack([sys_real, sys_imag], axis=2)
    incoming = jnp.zeros((NE, 2, dimension, dimension), jnp.float32)
    left_sigma = []
    for block_index in range(block_count):
        left_sigma.append(incoming)
        green_left = newton_inverse(system[:, block_index] - incoming)
        incoming = left_couple(coupling[block_index], green_left)
    arriving = jnp.zeros((NE, 2, dimension, dimension), jnp.float32)
    right_sigma = [None] * block_count
    for block_index in range(block_count - 1, -1, -1):
        self_energy = right_couple(coupling[block_index], arriving)
        right_sigma[block_index] = self_energy
        arriving = newton_inverse(system[:, block_index] - self_energy)
    green_list = []
    for block_index in range(block_count):
        green_list.append(newton_inverse((system[:, block_index] - left_sigma[block_index]) - right_sigma[block_index]))
    green = jnp.stack(green_list, axis=1)
    padded = jnp.pad(green, ((OMAX, OMAX), (0, 0), (0, 0), (0, 0), (0, 0)))
    local_sum = jnp.zeros(green.shape, jnp.float32)
    side_sum = jnp.zeros(green.shape, jnp.float32)
    for mode_index in range(MODES):
        begin = (phonon_shift[mode_index] + OMAX).astype(jnp.int32)
        shifted = lax.dynamic_slice_in_dim(padded, begin, NE, 0)
        local_sum = local_sum + phonon_local[mode_index] * shifted
        side_sum = side_sum + phonon_side[mode_index] * shifted
    side_pad = jnp.pad(side_sum, ((0, 0), (1, 1), (0, 0), (0, 0), (0, 0)))
    return local_sum + side_pad[:, :-2] + side_pad[:, 2:]
```

```python
import jax
import jax.numpy as jnp
from jax import lax
from jax.experimental import pallas as pl
from jax.experimental.pallas import tpu as pltpu
from jax.sharding import PartitionSpec as P

MODES = 4
N = 256
F32 = jnp.float32
BF16 = jnp.bfloat16
MESH = pl.DeviceIdType.MESH

ORDERS = ((2, 3, 7, 5, 6, 0), (2, 3, 5, 4, 7, 6), (5, 4, 2, 3, 6, 7), (5, 4, 6, 2, 7, 0))
SLOTS = 6


def order_code(digits):
    return sum(d * 8**i for i, d in enumerate(digits))


def cat(parts, axis):
    return jnp.concatenate(parts, axis=axis)


def split(x):
    hi = x.astype(BF16)
    return hi, (x - hi.astype(F32)).astype(BF16)


def dot3(a, b):
    return jnp.dot(
        cat([a[0], a[1], a[0]], 1), cat([b[0], b[0], b[1]], 0), preferred_element_type=F32
    )


def halves(re, im):
    return split(re), split(im), split(re + im)


def cdot(a, b):
    p1 = dot3(a[0], b[0])
    p2 = dot3(a[1], b[1])
    p3 = dot3(a[2], b[2])
    return p1 - p2, p3 - p1 - p2


def diagonal_mask():
    return lax.broadcasted_iota(jnp.int32, (N, N), 0) == lax.broadcasted_iota(jnp.int32, (N, N), 1)


def inverse(mr, mi):
    eye = diagonal_mask()

    def reciprocal(axis):
        dr = jnp.sum(jnp.where(eye, mr, 0.0), axis=axis, keepdims=True)
        di = jnp.sum(jnp.where(eye, mi, 0.0), axis=axis, keepdims=True)
        modulus = dr * dr + di * di
        return dr / modulus, -di / modulus

    xr, xi = reciprocal(0)
    rr = jnp.where(eye, 0.0, mi * xi - mr * xr)
    ri = jnp.where(eye, 0.0, -(mr * xi + mi * xr))
    r = halves(rr, ri)
    sr, si = cdot(r, r)
    s = halves(sr, si)
    tr, ti = cdot(s, s)
    yr = jnp.where(eye, 1.0, rr)
    ur, ui = cdot(halves(yr, ri), s)
    yr = yr + ur
    yi = ri + ui
    ur, ui = cdot(halves(yr, yi), halves(tr, ti))
    yr = yr + ur
    yi = yi + ui
    cr, ci = reciprocal(1)
    return yr * cr - yi * ci, yr * ci + yi * cr


def couple(a, gr, gi, b):
    gr, gi = split(gr), split(gi)
    g = (cat([gr[0], gi[0]], 1), cat([gr[1], gi[1]], 1))
    hi, lo = split(dot3(a, g))
    hi = cat([hi[:, :N], hi[:, N:]], 0)
    lo = cat([lo[:, :N], lo[:, N:]], 0)
    both = dot3((hi, lo), b)
    return both[:N], both[N:]


def kernel(
    onsite, hop, coup, broad, born, shift, ploc, pside, out,
    system, links, sig, green, hp, hm, ho, hf, wl, ws, ls, ss, sin,
    chain_s, chain_r, y_s, y_r, o_s, o_r, f_s, f_r, side_s, side_r, go,
):
    e = lax.axis_index("energy")
    s = lax.axis_index("section")
    core = lax.rem(e, 2)
    other = e + 1 - 2 * core
    has_p = e < 30
    has_m = e >= 2
    has_right = s < 3
    has_left = s > 0

    barrier = pltpu.get_barrier_semaphore()

    def greet(cond, where):
        @pl.when(cond)
        def _():
            pl.semaphore_signal(barrier, inc=1, device_id=where, device_id_type=MESH)

    greet(has_right, {"section": lax.rem(s + 1, 4)})
    greet(has_left, {"section": lax.rem(s + 3, 4)})
    greet(has_p, {"energy": lax.rem(e + 2, 32)})
    greet(has_m, {"energy": lax.rem(e + 30, 32)})
    pl.semaphore_signal(barrier, inc=1, device_id={"energy": other}, device_id_type=MESH)

    def remote(src, dst, ssem, rsem, where):
        return pltpu.make_async_remote_copy(
            src_ref=src, dst_ref=dst, send_sem=ssem, recv_sem=rsem, device_id=where, device_id_type=MESH
        )

    def left_copy():
        return remote(sig.at[5], sig.at[1], chain_s.at[0], chain_r.at[0], {"section": lax.rem(s + 1, 4)})

    def right_copy():
        return remote(green.at[2], sig.at[6], chain_s.at[1], chain_r.at[1], {"section": lax.rem(s + 3, 4)})

    def y_copy(up, b, part):
        if up:
            return remote(green.at[b, part], hm.at[b, part], y_s.at[0, b, part], y_r.at[0, b, part],
                          {"energy": lax.rem(e + 2, 32)})
        return remote(green.at[b, part], hp.at[b, part], y_s.at[1, b, part], y_r.at[1, b, part],
                      {"energy": lax.rem(e + 30, 32)})

    def own_copy(b, part):
        return remote(green.at[b, part], ho.at[b, part], o_s.at[b, part], o_r.at[b, part], {"energy": other})

    def fwd_copy(src, b, part):
        return remote(src.at[b, part], hf.at[b, part], f_s.at[b, part], f_r.at[b, part], {"energy": other})

    def side_right():
        return remote(ss.at[1], sin.at[0], side_s.at[1], side_r.at[0], {"section": lax.rem(s + 1, 4)})

    def side_left():
        return remote(ss.at[0], sin.at[1], side_s.at[0], side_r.at[1], {"section": lax.rem(s + 3, 4)})

    energy = -2.0 + 4.0 * e.astype(F32) / 31.0
    eta = broad[0]

    def setup(b, carry):
        eye = diagonal_mask()
        h = hop[b]
        ham = 0.5 * (h + h.T)
        system[b, 0] = jnp.where(eye, energy - onsite[pl.ds(b, 1), :], 0.0) - ham - born[0, b, 0]
        system[b, 1] = jnp.where(eye, eta, 0.0) - born[0, b, 1]
        v = coup[b]
        vh, vl = split(v)
        links[b, 0] = vh
        links[b, 1] = vl
        vh, vl = split(v.T)
        links[b, 2] = vh
        links[b, 3] = vl
        return carry

    lax.fori_loop(0, 2, setup, 0)
    sig[0] = jnp.zeros((2, N, N), F32)

    @pl.when(s == 0)
    def _():
        sig[1] = jnp.zeros((2, N, N), F32)

    @pl.when(s == 3)
    def _():
        sig[4] = jnp.zeros((2, N, N), F32)

    partners = (
        1 + has_right.astype(jnp.int32) + has_left.astype(jnp.int32)
        + has_p.astype(jnp.int32) + has_m.astype(jnp.int32)
    )
    pl.semaphore_wait(barrier, partners)

    def weights():
        def one(d, carry):
            wloc = jnp.zeros((N, N), F32)
            wside = jnp.zeros((N, N), F32)
            for k in range(MODES):
                on = jnp.where(shift[k] == d - 2, 1.0, 0.0)
                wloc = wloc + on * ploc[k]
                wside = wside + on * pside[k]
            wl[d] = wloc
            ws[d] = wside
            return carry

        lax.fori_loop(0, 5, one, 0)

    def at_section(values):
        return jnp.where(s == 0, values[0], jnp.where(s == 1, values[1], jnp.where(s == 2, values[2], values[3])))

    def slot(i, code):
        digit = lax.rem(code, 8)
        kind = digit // 2
        b = lax.rem(digit, 2)

        @pl.when(i == at_section((2, 0, 0, 2)))
        def _():
            weights()

        @pl.when(i == at_section((7, 0, 2, 2)))
        def _():
            left_copy().wait_recv()

        @pl.when(i == at_section((2, 2, 0, 7)))
        def _():
            right_copy().wait_recv()
            re, im = couple((links[1, 0], links[1, 1]), sig[6, 0], sig[6, 1], (links[1, 2], links[1, 3]))
            sig[4, 0] = re
            sig[4, 1] = im

        @pl.when(kind > 0)
        def _():
            first = jnp.where(kind == 2, 0, 1 + b)
            second = jnp.where(kind == 1, 0, 3 + b)
            place = jnp.where(kind == 3, b, jnp.where(digit == 4, 2, 3))
            re, im = inverse(
                system[b, 0] - sig[first, 0] - sig[second, 0], system[b, 1] - sig[first, 1] - sig[second, 1]
            )
            green[place, 0] = re
            green[place, 1] = im

            @pl.when((kind == 1) | (digit == 5))
            def _():
                v = jnp.where(kind == 1, b, 0)
                a0 = jnp.where(kind == 1, 2, 0)
                b0 = 2 - a0
                target = jnp.where(digit == 2, 2, jnp.where(digit == 3, 5, 3))
                re, im = couple((links[v, a0], links[v, a0 + 1]), green[3, 0], green[3, 1],
                                (links[v, b0], links[v, b0 + 1]))
                sig[target, 0] = re
                sig[target, 1] = im

            @pl.when((i == 1) & ((s == 0) | (s == 3)) & (core == 1))
            def _():
                pl.semaphore_wait(go, 1)

            @pl.when(digit == 3)
            def _():
                left_copy().start()

            @pl.when(digit == 4)
            def _():
                right_copy().start()

            @pl.when((i == 1) & (core == 0))
            def _():
                @pl.when(s == 0)
                def _():
                    left_copy().wait_send()

                @pl.when(s == 3)
                def _():
                    right_copy().wait_send()

                @pl.when((s == 0) | (s == 3))
                def _():
                    pl.semaphore_signal(go, inc=1, device_id={"energy": other}, device_id_type=MESH)

            @pl.when(kind == 3)
            def _():
                for part in range(2):
                    @pl.when(has_p)
                    def _():
                        y_copy(True, b, part).start()

                    @pl.when(has_m)
                    def _():
                        y_copy(False, b, part).start()

                    own_copy(b, part).start()

        return code // 8

    lax.fori_loop(0, SLOTS, slot, at_section([order_code(d) for d in ORDERS]))

    def units(t, carry):
        first = jnp.where(s < 2, 1, 0)
        half = t // 2
        b = first + half - 2 * first * half
        part = lax.rem(t, 2)

        def add(source, d):
            x = source[b, part]
            ls[b, part] = ls[b, part] + wl[d] * x
            ss[b, part] = ss[b, part] + ws[d] * x

        x = green[b, part]
        ls[b, part] = wl[2] * x
        ss[b, part] = ws[2] * x
        own_copy(b, part).wait_recv()
        add(ho, 3 - 2 * core)

        @pl.when(has_p)
        def _():
            y_copy(False, b, part).wait_recv()

            @pl.when(core == 0)
            def _():
                fwd_copy(hp, b, part).start()

            add(hp, 4)

        @pl.when(has_m)
        def _():
            y_copy(True, b, part).wait_recv()

            @pl.when(core == 1)
            def _():
                fwd_copy(hm, b, part).start()

            add(hm, 0)

        @pl.when(((core == 0) & has_m) | ((core == 1) & has_p))
        def _():
            fwd_copy(hp, b, part).wait_recv()
            add(hf, 1 + 2 * core)

        @pl.when(part == 1)
        def _():
            @pl.when((b == 1) & has_right)
            def _():
                side_right().start()

            @pl.when((b == 0) & has_left)
            def _():
                side_left().start()

        return carry

    lax.fori_loop(0, 4, units, 0)

    for b in range(2):
        for part in range(2):
            out[0, b, part] = ls[b, part] + ss[1 - b, part]

    @pl.when(has_left)
    def _():
        side_right().wait_recv()
        for part in range(2):
            out[0, 0, part] = out[0, 0, part] + sin[0, part]

    @pl.when(has_right)
    def _():
        side_left().wait_recv()
        for part in range(2):
            out[0, 1, part] = out[0, 1, part] + sin[1, part]

    @pl.when(has_right)
    def _():
        side_right().wait_send()

        @pl.when((s > 0) | (core == 1))
        def _():
            left_copy().wait_send()

    @pl.when(has_left)
    def _():
        side_left().wait_send()

        @pl.when((s < 3) | (core == 1))
        def _():
            right_copy().wait_send()

    for b in range(2):
        for part in range(2):
            own_copy(b, part).wait_send()

            @pl.when(has_p)
            def _():
                y_copy(True, b, part).wait_send()

            @pl.when(has_m)
            def _():
                y_copy(False, b, part).wait_send()

            @pl.when(((core == 0) & has_p) | ((core == 1) & has_m))
            def _():
                fwd_copy(hp, b, part).wait_send()


def local(onsite, hopping, coupling, broadening, born_sigma, phonon_shift, phonon_local, phonon_side):
    vmem = pl.BlockSpec(memory_space=pltpu.VMEM)
    smem = pl.BlockSpec(memory_space=pltpu.SMEM)
    dma = pltpu.SemaphoreType.DMA
    block = (2, N, N)
    pair = (2, 2, N, N)
    return pl.pallas_call(
        kernel,
        out_shape=jax.ShapeDtypeStruct(born_sigma.shape, F32),
        in_specs=[vmem, vmem, vmem, smem, vmem, smem, vmem, vmem],
        out_specs=vmem,
        scratch_shapes=[
            pltpu.VMEM(pair, F32),
            pltpu.VMEM((2, 4, N, N), BF16),
            pltpu.VMEM((7,) + block, F32),
            pltpu.VMEM((4,) + block, F32),
            pltpu.VMEM(pair, F32),
            pltpu.VMEM(pair, F32),
            pltpu.VMEM(pair, F32),
            pltpu.VMEM(pair, F32),
            pltpu.VMEM((5, N, N), F32),
            pltpu.VMEM((5, N, N), F32),
            pltpu.VMEM(pair, F32),
            pltpu.VMEM(pair, F32),
            pltpu.VMEM(pair, F32),
            dma((2,)), dma((2,)),
            dma((2, 2, 2)), dma((2, 2, 2)),
            dma((2, 2)), dma((2, 2)),
            dma((2, 2)), dma((2, 2)),
            dma((2,)), dma((2,)),
            pltpu.SemaphoreType.REGULAR,
        ],
        compiler_params=pltpu.CompilerParams(
            collective_id=0, has_side_effects=True, vmem_limit_bytes=56 * 2**20
        ),
        cost_estimate=pl.CostEstimate(flops=6 * 60 * 2 * N**3, bytes_accessed=6 * 2**20, transcendentals=0),
    )(onsite, hopping, coupling, broadening, born_sigma, phonon_shift, phonon_local, phonon_side)


def solution(mesh):
    in_specs = (
        P("section", None),
        P("section", None, None),
        P("section", None, None),
        P("energy"),
        P("energy", "section", None, None, None),
        P(),
        P(),
        P(),
    )
    out_specs = P("energy", "section", None, None, None)
    return jax.shard_map(local, mesh=mesh, in_specs=in_specs, out_specs=out_specs, check_vma=False)
```

```python
import jax
import jax.numpy as jnp
from jax import lax
from jax.experimental import pallas as pl
from jax.experimental.pallas import tpu as pltpu
from jax.sharding import PartitionSpec as P

MODES = 4
N = 256
F32 = jnp.float32
BF16 = jnp.bfloat16
MESH = pl.DeviceIdType.MESH

ORDERS = ((2, 3, 7, 5, 6, 0), (2, 3, 5, 4, 7, 6), (5, 4, 2, 3, 6, 7), (5, 4, 6, 2, 7, 0))
SLOTS = 6


def order_code(digits):
    return sum(d * 8**i for i, d in enumerate(digits))


def cat(parts, axis):
    return jnp.concatenate(parts, axis=axis)


def split(x):
    hi = x.astype(BF16)
    return hi, (x - hi.astype(F32)).astype(BF16)


def dot3(a, b):
    return jnp.dot(
        cat([a[0], a[1], a[0]], 1), cat([b[0], b[0], b[1]], 0), preferred_element_type=F32
    )


def halves(re, im):
    return split(re), split(im), split(re + im)


def cdot(a, b):
    p1 = dot3(a[0], b[0])
    p2 = dot3(a[1], b[1])
    p3 = dot3(a[2], b[2])
    return p1 - p2, p3 - p1 - p2


def diagonal_mask():
    return lax.broadcasted_iota(jnp.int32, (N, N), 0) == lax.broadcasted_iota(jnp.int32, (N, N), 1)


def inverse(mr, mi):
    eye = diagonal_mask()

    def reciprocal(axis):
        dr = jnp.sum(jnp.where(eye, mr, 0.0), axis=axis, keepdims=True)
        di = jnp.sum(jnp.where(eye, mi, 0.0), axis=axis, keepdims=True)
        modulus = dr * dr + di * di
        return dr / modulus, -di / modulus

    xr, xi = reciprocal(0)
    rr = jnp.where(eye, 0.0, mi * xi - mr * xr)
    ri = jnp.where(eye, 0.0, -(mr * xi + mi * xr))
    r = halves(rr, ri)
    sr, si = cdot(r, r)
    s = halves(sr, si)
    tr, ti = cdot(s, s)
    yr = jnp.where(eye, 1.0, rr)
    ur, ui = cdot(halves(yr, ri), s)
    yr = yr + ur
    yi = ri + ui
    ur, ui = cdot(halves(yr, yi), halves(tr, ti))
    yr = yr + ur
    yi = yi + ui
    cr, ci = reciprocal(1)
    return yr * cr - yi * ci, yr * ci + yi * cr


def couple(a, gr, gi, b):
    gr, gi = split(gr), split(gi)
    g = (cat([gr[0], gi[0]], 1), cat([gr[1], gi[1]], 1))
    hi, lo = split(dot3(a, g))
    hi = cat([hi[:, :N], hi[:, N:]], 0)
    lo = cat([lo[:, :N], lo[:, N:]], 0)
    both = dot3((hi, lo), b)
    return both[:N], both[N:]


def kernel(
    onsite, hop, coup, broad, born, shift, ploc, pside, out,
    system, links, sig, green, hp, hm, ho, hf, wl, ws, ls, ss, sin,
    chain_s, chain_r, y_s, y_r, o_s, o_r, f_s, f_r, side_s, side_r, go,
):
    e = lax.axis_index("energy")
    s = lax.axis_index("section")
    core = lax.rem(e, 2)
    other = e + 1 - 2 * core
    has_p = e < 30
    has_m = e >= 2
    has_right = s < 3
    has_left = s > 0
    early = jnp.where(s < 2, 1, 0)

    barrier = pltpu.get_barrier_semaphore()

    def greet(cond, where):
        @pl.when(cond)
        def _():
            pl.semaphore_signal(barrier, inc=1, device_id=where, device_id_type=MESH)

    greet(has_right, {"section": lax.rem(s + 1, 4)})
    greet(has_left, {"section": lax.rem(s + 3, 4)})
    greet(has_p, {"energy": lax.rem(e + 2, 32)})
    greet(has_m, {"energy": lax.rem(e + 30, 32)})
    pl.semaphore_signal(barrier, inc=1, device_id={"energy": other}, device_id_type=MESH)

    def remote(src, dst, ssem, rsem, where):
        return pltpu.make_async_remote_copy(
            src_ref=src, dst_ref=dst, send_sem=ssem, recv_sem=rsem, device_id=where, device_id_type=MESH
        )

    def left_copy():
        return remote(sig.at[5], sig.at[1], chain_s.at[0], chain_r.at[0], {"section": lax.rem(s + 1, 4)})

    def right_copy():
        return remote(green.at[2], sig.at[6], chain_s.at[1], chain_r.at[1], {"section": lax.rem(s + 3, 4)})

    def y_copy(up, b, part):
        if up:
            return remote(green.at[b, part], hm.at[b, part], y_s.at[0, b, part], y_r.at[0, b, part],
                          {"energy": lax.rem(e + 2, 32)})
        return remote(green.at[b, part], hp.at[b, part], y_s.at[1, b, part], y_r.at[1, b, part],
                      {"energy": lax.rem(e + 30, 32)})

    def own_copy(b, part):
        return remote(green.at[b, part], ho.at[b, part], o_s.at[b, part], o_r.at[b, part], {"energy": other})

    def send_block(b):
        for part in range(2):
            @pl.when(has_p)
            def _():
                y_copy(True, b, part).start()

            @pl.when(has_m)
            def _():
                y_copy(False, b, part).start()

    def fwd_copy(src, b, part):
        return remote(src.at[b, part], hf.at[b, part], f_s.at[b, part], f_r.at[b, part], {"energy": other})

    def side_right(part):
        return remote(ss.at[1, part], sin.at[0, part], side_s.at[1, part], side_r.at[0, part],
                      {"section": lax.rem(s + 1, 4)})

    def side_left(part):
        return remote(ss.at[0, part], sin.at[1, part], side_s.at[0, part], side_r.at[1, part],
                      {"section": lax.rem(s + 3, 4)})

    energy = -2.0 + 4.0 * e.astype(F32) / 31.0
    eta = broad[0]

    def setup(b, carry):
        eye = diagonal_mask()
        h = hop[b]
        ham = 0.5 * (h + h.T)
        system[b, 0] = jnp.where(eye, energy - onsite[pl.ds(b, 1), :], 0.0) - ham - born[0, b, 0]
        system[b, 1] = jnp.where(eye, eta, 0.0) - born[0, b, 1]
        v = coup[b]
        vh, vl = split(v)
        links[b, 0] = vh
        links[b, 1] = vl
        vh, vl = split(v.T)
        links[b, 2] = vh
        links[b, 3] = vl
        return carry

    lax.fori_loop(0, 2, setup, 0)
    sig[0] = jnp.zeros((2, N, N), F32)

    @pl.when(s == 0)
    def _():
        sig[1] = jnp.zeros((2, N, N), F32)

    @pl.when(s == 3)
    def _():
        sig[4] = jnp.zeros((2, N, N), F32)

    partners = (
        1 + has_right.astype(jnp.int32) + has_left.astype(jnp.int32)
        + has_p.astype(jnp.int32) + has_m.astype(jnp.int32)
    )
    pl.semaphore_wait(barrier, partners)

    def weights():
        def one(d, carry):
            wloc = jnp.zeros((N, N), F32)
            wside = jnp.zeros((N, N), F32)
            for k in range(MODES):
                on = jnp.where(shift[k] == d - 2, 1.0, 0.0)
                wloc = wloc + on * ploc[k]
                wside = wside + on * pside[k]
            wl[d] = wloc
            ws[d] = wside
            return carry

        lax.fori_loop(0, 5, one, 0)

    def at_section(values):
        return jnp.where(s == 0, values[0], jnp.where(s == 1, values[1], jnp.where(s == 2, values[2], values[3])))

    def slot(i, code):
        digit = lax.rem(code, 8)
        kind = digit // 2
        b = lax.rem(digit, 2)

        @pl.when(i == at_section((2, 0, 0, 2)))
        def _():
            weights()

        @pl.when(i == at_section((7, 0, 2, 2)))
        def _():
            left_copy().wait_recv()

        @pl.when(i == at_section((2, 2, 0, 7)))
        def _():
            right_copy().wait_recv()
            re, im = couple((links[1, 0], links[1, 1]), sig[6, 0], sig[6, 1], (links[1, 2], links[1, 3]))
            sig[4, 0] = re
            sig[4, 1] = im

        @pl.when(kind > 0)
        def _():
            first = jnp.where(kind == 2, 0, 1 + b)
            second = jnp.where(kind == 1, 0, 3 + b)
            place = jnp.where(kind == 3, b, jnp.where(digit == 4, 2, 3))
            re, im = inverse(
                system[b, 0] - sig[first, 0] - sig[second, 0], system[b, 1] - sig[first, 1] - sig[second, 1]
            )
            green[place, 0] = re
            green[place, 1] = im

            @pl.when((kind == 1) | (digit == 5))
            def _():
                v = jnp.where(kind == 1, b, 0)
                a0 = jnp.where(kind == 1, 2, 0)
                b0 = 2 - a0
                target = jnp.where(digit == 2, 2, jnp.where(digit == 3, 5, 3))
                re, im = couple((links[v, a0], links[v, a0 + 1]), green[3, 0], green[3, 1],
                                (links[v, b0], links[v, b0 + 1]))
                sig[target, 0] = re
                sig[target, 1] = im

            @pl.when((i == 1) & ((s == 0) | (s == 3)) & (core == 1))
            def _():
                pl.semaphore_wait(go, 1)

            @pl.when(digit == 3)
            def _():
                left_copy().start()

            @pl.when(digit == 4)
            def _():
                right_copy().start()

            @pl.when((i == 1) & (core == 0))
            def _():
                @pl.when(s == 0)
                def _():
                    left_copy().wait_send()

                @pl.when(s == 3)
                def _():
                    right_copy().wait_send()

                @pl.when((s == 0) | (s == 3))
                def _():
                    pl.semaphore_signal(go, inc=1, device_id={"energy": other}, device_id_type=MESH)

            @pl.when(kind == 3)
            def _():
                for part in range(2):
                    own_copy(b, part).start()

                @pl.when(b == early)
                def _():
                    send_block(b)

        return code // 8

    lax.fori_loop(0, SLOTS, slot, at_section([order_code(d) for d in ORDERS]))

    def units(t, carry):
        half = t // 2
        b = early + half - 2 * early * half
        part = lax.rem(t, 2)

        @pl.when(t == 0)
        def _():
            send_block(1 - early)

        def add(source, d):
            x = source[b, part]
            ls[b, part] = ls[b, part] + wl[d] * x
            ss[b, part] = ss[b, part] + ws[d] * x

        x = green[b, part]
        ls[b, part] = wl[2] * x
        ss[b, part] = ws[2] * x
        own_copy(b, part).wait_recv()
        add(ho, 3 - 2 * core)

        @pl.when(has_p)
        def _():
            y_copy(False, b, part).wait_recv()

            @pl.when(core == 0)
            def _():
                fwd_copy(hp, b, part).start()

            add(hp, 4)

        @pl.when(has_m)
        def _():
            y_copy(True, b, part).wait_recv()

            @pl.when(core == 1)
            def _():
                fwd_copy(hm, b, part).start()

            add(hm, 0)

        @pl.when(((core == 0) & has_m) | ((core == 1) & has_p))
        def _():
            fwd_copy(hp, b, part).wait_recv()
            add(hf, 1 + 2 * core)

        @pl.when((b == 1) & has_right)
        def _():
            side_right(part).start()

        @pl.when((b == 0) & has_left)
        def _():
            side_left(part).start()

        return carry

    lax.fori_loop(0, 4, units, 0)

    for b in range(2):
        for part in range(2):
            out[0, b, part] = ls[b, part] + ss[1 - b, part]

    @pl.when(has_left)
    def _():
        for part in range(2):
            side_right(part).wait_recv()
            out[0, 0, part] = out[0, 0, part] + sin[0, part]

    @pl.when(has_right)
    def _():
        for part in range(2):
            side_left(part).wait_recv()
            out[0, 1, part] = out[0, 1, part] + sin[1, part]

    @pl.when(has_right)
    def _():
        for part in range(2):
            side_right(part).wait_send()

        @pl.when((s > 0) | (core == 1))
        def _():
            left_copy().wait_send()

    @pl.when(has_left)
    def _():
        for part in range(2):
            side_left(part).wait_send()

        @pl.when((s < 3) | (core == 1))
        def _():
            right_copy().wait_send()

    for b in range(2):
        for part in range(2):
            own_copy(b, part).wait_send()

            @pl.when(has_p)
            def _():
                y_copy(True, b, part).wait_send()

            @pl.when(has_m)
            def _():
                y_copy(False, b, part).wait_send()

            @pl.when(((core == 0) & has_p) | ((core == 1) & has_m))
            def _():
                fwd_copy(hp, b, part).wait_send()


def local(onsite, hopping, coupling, broadening, born_sigma, phonon_shift, phonon_local, phonon_side):
    vmem = pl.BlockSpec(memory_space=pltpu.VMEM)
    smem = pl.BlockSpec(memory_space=pltpu.SMEM)
    dma = pltpu.SemaphoreType.DMA
    block = (2, N, N)
    pair = (2, 2, N, N)
    return pl.pallas_call(
        kernel,
        out_shape=jax.ShapeDtypeStruct(born_sigma.shape, F32),
        in_specs=[vmem, vmem, vmem, smem, vmem, smem, vmem, vmem],
        out_specs=vmem,
        scratch_shapes=[
            pltpu.VMEM(pair, F32),
            pltpu.VMEM((2, 4, N, N), BF16),
            pltpu.VMEM((7,) + block, F32),
            pltpu.VMEM((4,) + block, F32),
            pltpu.VMEM(pair, F32),
            pltpu.VMEM(pair, F32),
            pltpu.VMEM(pair, F32),
            pltpu.VMEM(pair, F32),
            pltpu.VMEM((5, N, N), F32),
            pltpu.VMEM((5, N, N), F32),
            pltpu.VMEM(pair, F32),
            pltpu.VMEM(pair, F32),
            pltpu.VMEM(pair, F32),
            dma((2,)), dma((2,)),
            dma((2, 2, 2)), dma((2, 2, 2)),
            dma((2, 2)), dma((2, 2)),
            dma((2, 2)), dma((2, 2)),
            dma((2, 2)), dma((2, 2)),
            pltpu.SemaphoreType.REGULAR,
        ],
        compiler_params=pltpu.CompilerParams(
            collective_id=0, has_side_effects=True, vmem_limit_bytes=56 * 2**20
        ),
        cost_estimate=pl.CostEstimate(flops=6 * 60 * 2 * N**3, bytes_accessed=6 * 2**20, transcendentals=0),
    )(onsite, hopping, coupling, broadening, born_sigma, phonon_shift, phonon_local, phonon_side)


def solution(mesh):
    in_specs = (
        P("section", None),
        P("section", None, None),
        P("section", None, None),
        P("energy"),
        P("energy", "section", None, None, None),
        P(),
        P(),
        P(),
    )
    out_specs = P("energy", "section", None, None, None)
    return jax.shard_map(local, mesh=mesh, in_specs=in_specs, out_specs=out_specs, check_vma=False)
```

```python
import jax
import jax.numpy as jnp
from jax import lax
from jax.experimental import pallas as pl
from jax.experimental.pallas import tpu as pltpu
from jax.sharding import PartitionSpec as P

MODES = 4
N = 256
F32 = jnp.float32
BF16 = jnp.bfloat16
MESH = pl.DeviceIdType.MESH

L, R, G = 4, 8, 12
ORDERS = (
    ((L, L + 1, G + 1, R + 1, G), (L, L + 1, L + 2, L + 3, G + 1, R + 1, G),
     (R + 1, R, R + 3, R + 2, G, L, G + 1), (R + 1, R, G, L, G + 1)),
    ((L, L + 1, G + 1, R + 1, G), (L, L + 1, R + 1, R, G + 1, G),
     (R + 1, R, L, L + 1, G, G + 1), (R + 1, R, G, L, G + 1)),
)
SLOTS = 7
CUTS = 1
UNITS = 2 * CUTS
ROWS = N // CUTS


def order_code(steps):
    return sum(step * 16**i for i, step in enumerate(steps))


def cat(parts, axis):
    return jnp.concatenate(parts, axis=axis)


def split(x):
    hi = x.astype(BF16)
    return hi, (x - hi.astype(F32)).astype(BF16)


def dot3(a, b):
    return jnp.dot(
        cat([a[0], a[1], a[0]], 1), cat([b[0], b[0], b[1]], 0), preferred_element_type=F32
    )


def halves(re, im):
    return split(re), split(im), split(re + im)


def cdot(a, b):
    p1 = dot3(a[0], b[0])
    p2 = dot3(a[1], b[1])
    p3 = dot3(a[2], b[2])
    return p1 - p2, p3 - p1 - p2


def diagonal_mask():
    return lax.broadcasted_iota(jnp.int32, (N, N), 0) == lax.broadcasted_iota(jnp.int32, (N, N), 1)


def inverse(mr, mi):
    eye = diagonal_mask()

    def reciprocal(axis):
        dr = jnp.sum(jnp.where(eye, mr, 0.0), axis=axis, keepdims=True)
        di = jnp.sum(jnp.where(eye, mi, 0.0), axis=axis, keepdims=True)
        modulus = dr * dr + di * di
        return dr / modulus, -di / modulus

    xr, xi = reciprocal(0)
    rr = jnp.where(eye, 0.0, mi * xi - mr * xr)
    ri = jnp.where(eye, 0.0, -(mr * xi + mi * xr))
    r = halves(rr, ri)
    sr, si = cdot(r, r)
    s = halves(sr, si)
    tr, ti = cdot(s, s)
    ur, ui = cdot(r, s)
    yr = jnp.where(eye, 1.0, rr) + sr + ur
    yi = ri + si + ui
    ur, ui = cdot(halves(yr, yi), halves(tr, ti))
    yr = yr + ur
    yi = yi + ui
    cr, ci = reciprocal(1)
    return yr * cr - yi * ci, yr * ci + yi * cr


def couple(a, gr, gi, b):
    gr, gi = split(gr), split(gi)
    g = (cat([gr[0], gi[0]], 1), cat([gr[1], gi[1]], 1))
    hi, lo = split(dot3(a, g))
    hi = cat([hi[:, :N], hi[:, N:]], 0)
    lo = cat([lo[:, :N], lo[:, N:]], 0)
    both = dot3((hi, lo), b)
    return both[:N], both[N:]


def kernel(
    onsite, hop, coup, broad, born, shift, ploc, pside, out,
    system, links, sig, green, late, hp, hm, ho, hf, wl, ws, ls, ss, sin, fcoup,
    chain_s, chain_r, y_s, y_r, o_s, o_r, f_s, f_r, side_s, side_r, pre_s, pre_r, go,
):
    e = lax.axis_index("energy")
    s = lax.axis_index("section")
    core = lax.rem(e, 2)
    other = e + 1 - 2 * core
    has_p = e < 30
    has_m = e >= 2
    has_right = s < 3
    has_left = s > 0
    middle = (s == 1) | (s == 2)
    early = jnp.where(s < 2, 1, 0)

    barrier = pltpu.get_barrier_semaphore()

    def greet(cond, where):
        @pl.when(cond)
        def _():
            pl.semaphore_signal(barrier, inc=1, device_id=where, device_id_type=MESH)

    for distance in (1, 2, 3):
        pl.semaphore_signal(
            barrier, inc=1, device_id={"section": lax.rem(s + distance, 4)}, device_id_type=MESH
        )
    greet(has_p, {"energy": lax.rem(e + 2, 32)})
    greet(has_m, {"energy": lax.rem(e + 30, 32)})
    pl.semaphore_signal(barrier, inc=1, device_id={"energy": other}, device_id_type=MESH)

    def remote(src, dst, ssem, rsem, where):
        return pltpu.make_async_remote_copy(
            src_ref=src, dst_ref=dst, send_sem=ssem, recv_sem=rsem, device_id=where, device_id_type=MESH
        )

    def left_copy():
        return remote(sig.at[5], sig.at[1], chain_s.at[0], chain_r.at[0], {"section": lax.rem(s + 1, 4)})

    def right_copy():
        return remote(green.at[2], late.at[0], chain_s.at[1], chain_r.at[1], {"section": lax.rem(s + 3, 4)})

    def far_left_copy():
        return remote(sig.at[8], sig.at[1], chain_s.at[2], chain_r.at[0], {"section": lax.rem(s + 2, 4)})

    def far_right_copy():
        return remote(green.at[4], late.at[0], chain_s.at[2], chain_r.at[1], {"section": lax.rem(s + 2, 4)})

    swap = {"section": lax.rem(7 - s, 4)}

    def system_copy(b):
        return remote(system.at[b], system.at[2 + b], pre_s.at[b], pre_r.at[b], swap)

    def coupling_copy():
        return remote(coup, fcoup, pre_s.at[2], pre_r.at[2], swap)

    def y_copy(up, b, part):
        if up:
            return remote(green.at[b, part], hm.at[b, part], y_s.at[0, b, part], y_r.at[0, b, part],
                          {"energy": lax.rem(e + 2, 32)})
        return remote(green.at[b, part], hp.at[b, part], y_s.at[1, b, part], y_r.at[1, b, part],
                      {"energy": lax.rem(e + 30, 32)})

    def own_copy(b, part):
        return remote(green.at[b, part], ho.at[b, part], o_s.at[b, part], o_r.at[b, part], {"energy": other})

    def send_block(b):
        for part in range(UNITS):
            @pl.when(has_p)
            def _():
                y_copy(True, b, part).start()

            @pl.when(has_m)
            def _():
                y_copy(False, b, part).start()

    def fwd_copy(src, b, part):
        return remote(src.at[b, part], hf.at[b, part], f_s.at[b, part], f_r.at[b, part], {"energy": other})

    def side_right(part):
        return remote(ss.at[1, part], sin.at[0, part], side_s.at[1, part], side_r.at[0, part],
                      {"section": lax.rem(s + 1, 4)})

    def side_left(part):
        return remote(ss.at[0, part], sin.at[1, part], side_s.at[0, part], side_r.at[1, part],
                      {"section": lax.rem(s + 3, 4)})

    energy = -2.0 + 4.0 * e.astype(F32) / 31.0
    eta = broad[0]

    def link_halves(v, place):
        vh, vl = split(v)
        links[place, 0] = vh
        links[place, 1] = vl
        vh, vl = split(v.T)
        links[place, 2] = vh
        links[place, 3] = vl

    def setup(b, carry):
        eye = diagonal_mask()
        h = hop[b]
        ham = 0.5 * (h + h.T)
        system[b, 0] = jnp.where(eye, energy - onsite[pl.ds(b, 1), :], 0.0) - ham - born[0, b, 0]
        system[b, 1] = jnp.where(eye, eta, 0.0) - born[0, b, 1]
        link_halves(coup[b], b)
        return carry

    lax.fori_loop(0, 2, setup, 0)
    sig[0] = jnp.zeros((2, N, N), F32)

    @pl.when(s == 0)
    def _():
        sig[1] = jnp.zeros((2, N, N), F32)

    @pl.when(s == 3)
    def _():
        sig[4] = jnp.zeros((2, N, N), F32)

    def everyone_is_in():
        pl.semaphore_wait(barrier, 4 + has_p.astype(jnp.int32) + has_m.astype(jnp.int32))

    def weights():
        def one(d, carry):
            wloc = jnp.zeros((N, N), F32)
            wside = jnp.zeros((N, N), F32)
            for k in range(MODES):
                on = jnp.where(shift[k] == d - 2, 1.0, 0.0)
                wloc = wloc + on * ploc[k]
                wside = wside + on * pside[k]
            wl[d] = wloc.reshape(CUTS, ROWS, N)
            ws[d] = wside.reshape(CUTS, ROWS, N)
            return carry

        lax.fori_loop(0, 5, one, 0)

    first_block = lax.rem(s, 2)
    last_block = 1 - first_block

    @pl.when(middle)
    def _():
        everyone_is_in()

    @pl.when(middle & (core == 0))
    def _():
        coupling_copy().start()
        system_copy(first_block).start()

    @pl.when(middle)
    def _():
        weights()

    @pl.when(middle & (core == 0))
    def _():
        coupling_copy().wait_recv()

        def foreign(b, carry):
            link_halves(fcoup[b], 2 + b)
            return carry

        lax.fori_loop(0, 2, foreign, 0)
        coupling_copy().wait_send()
        system_copy(last_block).start()

    def pick(b, values):
        return jnp.where(b == 0, values[0], jnp.where(b == 1, values[1], jnp.where(b == 2, values[2], values[3])))

    def slot(i, code):
        digit = lax.rem(code, 16)
        kind = digit // 4
        b = lax.rem(digit, 4)
        is_l = kind == 1
        is_r = kind == 2

        @pl.when((i == 2) & jnp.logical_not(middle))
        def _():
            weights()

        @pl.when(i == pick(s, (9, 0, 4 - 2 * core, 2)))
        def _():
            left_copy().wait_recv()

        @pl.when(i == pick(s, (2, 4 - 2 * core, 0, 9)))
        def _():
            right_copy().wait_recv()
            re, im = couple((links[1, 0], links[1, 1]), late[0, :CUTS].reshape(N, N), late[0, CUTS:].reshape(N, N), (links[1, 2], links[1, 3]))
            sig[4, 0] = re
            sig[4, 1] = im

        @pl.when(kind > 0)
        def _():
            @pl.when(b >= 2)
            def _():
                system_copy(b - 2).wait_recv()

            first = jnp.where(is_r, 0, pick(b, (1, 2, 5, 7)))
            second = jnp.where(is_l, 0, pick(b, (3, 4, 8, 7)))
            place = jnp.where(kind == 3, b, jnp.where(is_r, pick(b, (2, 3, 4, 3)), 3))
            re, im = inverse(
                system[b, 0] - sig[first, 0] - sig[second, 0], system[b, 1] - sig[first, 1] - sig[second, 1]
            )
            green[place, :CUTS] = re.reshape(CUTS, ROWS, N)
            green[place, CUTS:] = im.reshape(CUTS, ROWS, N)

            at_end = (i == 1) & jnp.logical_not(middle)

            @pl.when(at_end)
            def _():
                everyone_is_in()

            @pl.when(at_end & (s == 3) & (core == 1))
            def _():
                pl.semaphore_wait(go, 1)

            @pl.when(is_r & (b == 0))
            def _():
                right_copy().start()

            @pl.when(is_r & (b == 2))
            def _():
                far_right_copy().start()

            @pl.when(is_l | (is_r & ((b == 1) | (b == 3) | ((b == 0) & (s == 2) & (core == 0)))))
            def _():
                v = jnp.where(is_l, b, pick(b, (3, 0, 0, 2)))
                a0 = jnp.where(is_l, 2, 0)
                b0 = 2 - a0
                target = jnp.where(is_l, pick(b, (2, 5, 7, 8)), pick(b, (7, 3, 0, 8)))
                re, im = couple((links[v, a0], links[v, a0 + 1]), green[place, :CUTS].reshape(N, N), green[place, CUTS:].reshape(N, N),
                                (links[v, b0], links[v, b0 + 1]))
                sig[target, 0] = re
                sig[target, 1] = im

            @pl.when(at_end & (s == 0) & (core == 1))
            def _():
                pl.semaphore_wait(go, 1)

            @pl.when(is_l & (b == 1))
            def _():
                left_copy().start()

            @pl.when(is_l & (b == 3))
            def _():
                far_left_copy().start()

            @pl.when(at_end & (core == 0))
            def _():
                @pl.when(s == 0)
                def _():
                    left_copy().wait_send()

                @pl.when(s == 3)
                def _():
                    right_copy().wait_send()

                pl.semaphore_signal(go, inc=1, device_id={"energy": other}, device_id_type=MESH)

            @pl.when(kind == 3)
            def _():
                for part in range(UNITS):
                    own_copy(b, part).start()

                @pl.when(b == early)
                def _():
                    send_block(b)

        return code // 16

    codes = [pick(s, [order_code(x) for x in orders]) for orders in ORDERS]
    lax.fori_loop(0, SLOTS, slot, jnp.where(core == 0, codes[0], codes[1]))

    def units(t, carry):
        half = t // UNITS
        b = early + half - 2 * early * half
        part = lax.rem(t, UNITS)
        rows = lax.rem(t, CUTS)

        @pl.when(t == 0)
        def _():
            send_block(1 - early)

        def add(source, d):
            x = source[b, part]
            ls[b, part] = ls[b, part] + wl[d, rows] * x
            ss[b, part] = ss[b, part] + ws[d, rows] * x

        x = green[b, part]
        ls[b, part] = wl[2, rows] * x
        ss[b, part] = ws[2, rows] * x
        own_copy(b, part).wait_recv()
        add(ho, 3 - 2 * core)

        @pl.when(has_p)
        def _():
            y_copy(False, b, part).wait_recv()

            @pl.when(core == 0)
            def _():
                fwd_copy(hp, b, part).start()

            add(hp, 4)

        @pl.when(has_m)
        def _():
            y_copy(True, b, part).wait_recv()

            @pl.when(core == 1)
            def _():
                fwd_copy(hm, b, part).start()

            add(hm, 0)

        @pl.when(((core == 0) & has_m) | ((core == 1) & has_p))
        def _():
            fwd_copy(hp, b, part).wait_recv()
            add(hf, 1 + 2 * core)

        @pl.when((b == 1) & has_right)
        def _():
            side_right(part).start()

        @pl.when((b == 0) & has_left)
        def _():
            side_left(part).start()

        return carry

    lax.fori_loop(0, 2 * UNITS, units, 0)

    def finish(t, carry):
        b = t // UNITS
        part = lax.rem(t, UNITS)

        @pl.when((b == 0) & has_left)
        def _():
            side_right(part).wait_recv()

        @pl.when((b == 1) & has_right)
        def _():
            side_left(part).wait_recv()

        away = jnp.where(jnp.where(b == 0, has_left, has_right), sin[b, part], 0.0)
        rows = pl.ds(pl.multiple_of(lax.rem(t, CUTS) * ROWS, ROWS), ROWS)
        out[0, b, part // CUTS, rows, :] = ls[b, part] + ss[1 - b, part] + away
        return carry

    lax.fori_loop(0, 2 * UNITS, finish, 0)

    @pl.when(has_right)
    def _():
        for part in range(UNITS):
            side_right(part).wait_send()

        @pl.when((s == 1) | (core == 1))
        def _():
            left_copy().wait_send()

    @pl.when(has_left)
    def _():
        for part in range(UNITS):
            side_left(part).wait_send()

        @pl.when((s == 2) | (core == 1))
        def _():
            right_copy().wait_send()

    @pl.when(middle & (core == 0))
    def _():
        far_left_copy().wait_send()
        system_copy(first_block).wait_send()
        system_copy(last_block).wait_send()

    for b in range(2):
        for part in range(UNITS):
            own_copy(b, part).wait_send()

            @pl.when(has_p)
            def _():
                y_copy(True, b, part).wait_send()

            @pl.when(has_m)
            def _():
                y_copy(False, b, part).wait_send()

            @pl.when(((core == 0) & has_p) | ((core == 1) & has_m))
            def _():
                fwd_copy(hp, b, part).wait_send()


def local(onsite, hopping, coupling, broadening, born_sigma, phonon_shift, phonon_local, phonon_side):
    vmem = pl.BlockSpec(memory_space=pltpu.VMEM)
    smem = pl.BlockSpec(memory_space=pltpu.SMEM)
    dma = pltpu.SemaphoreType.DMA
    block = (2, N, N)
    pieces = (UNITS, ROWS, N)
    return pl.pallas_call(
        kernel,
        out_shape=jax.ShapeDtypeStruct(born_sigma.shape, F32),
        in_specs=[vmem, vmem, vmem, smem, vmem, smem, vmem, vmem],
        out_specs=vmem,
        scratch_shapes=[
            pltpu.VMEM((4,) + block, F32),
            pltpu.VMEM((4, 4, N, N), BF16),
            pltpu.VMEM((9,) + block, F32),
            pltpu.VMEM((5,) + pieces, F32),
            pltpu.VMEM((1,) + pieces, F32),
            pltpu.VMEM((2,) + pieces, F32),
            pltpu.VMEM((2,) + pieces, F32),
            pltpu.VMEM((2,) + pieces, F32),
            pltpu.VMEM((2,) + pieces, F32),
            pltpu.VMEM((5, CUTS, ROWS, N), F32),
            pltpu.VMEM((5, CUTS, ROWS, N), F32),
            pltpu.VMEM((2,) + pieces, F32),
            pltpu.VMEM((2,) + pieces, F32),
            pltpu.VMEM((2,) + pieces, F32),
            pltpu.VMEM(block, F32),
            dma((3,)), dma((2,)),
            dma((2, 2, UNITS)), dma((2, 2, UNITS)),
            dma((2, UNITS)), dma((2, UNITS)),
            dma((2, UNITS)), dma((2, UNITS)),
            dma((2, UNITS)), dma((2, UNITS)),
            dma((3,)), dma((3,)),
            pltpu.SemaphoreType.REGULAR,
        ],
        compiler_params=pltpu.CompilerParams(
            collective_id=0, has_side_effects=True, vmem_limit_bytes=56 * 2**20
        ),
        cost_estimate=pl.CostEstimate(flops=6 * 60 * 2 * N**3, bytes_accessed=6 * 2**20, transcendentals=0),
    )(onsite, hopping, coupling, broadening, born_sigma, phonon_shift, phonon_local, phonon_side)


def solution(mesh):
    in_specs = (
        P("section", None),
        P("section", None, None),
        P("section", None, None),
        P("energy"),
        P("energy", "section", None, None, None),
        P(),
        P(),
        P(),
    )
    out_specs = P("energy", "section", None, None, None)
    return jax.shard_map(local, mesh=mesh, in_specs=in_specs, out_specs=out_specs, check_vma=False)
```

```python
import jax
import jax.numpy as jnp
from jax import lax
from jax.experimental import pallas as pl
from jax.experimental.pallas import tpu as pltpu
from jax.sharding import PartitionSpec as P

MODES = 4
N = 256
F32 = jnp.float32
BF16 = jnp.bfloat16
MESH = pl.DeviceIdType.MESH

L, R, G = 4, 8, 12
ORDERS = (
    ((L, L + 1, G + 1, R + 1, G), (L, L + 1, L + 2, L + 3, G + 1, R + 1, G),
     (R + 1, R, R + 3, R + 2, G, L, G + 1), (R + 1, R, G, L, G + 1)),
    ((L, L + 1, G + 1, R + 1, G), (L, L + 1, R + 1, R, G + 1, G),
     (R + 1, R, L, L + 1, G, G + 1), (R + 1, R, G, L, G + 1)),
)
SLOTS = 7
CUTS = 1
UNITS = 2 * CUTS
ROWS = N // CUTS


def order_code(steps):
    return sum(step * 16**i for i, step in enumerate(steps))


def cat(parts, axis):
    return jnp.concatenate(parts, axis=axis)


def split(x):
    hi = x.astype(BF16)
    return hi, (x - hi.astype(F32)).astype(BF16)


def dot3(a, b):
    return jnp.dot(
        cat([a[0], a[1], a[0]], 1), cat([b[0], b[0], b[1]], 0), preferred_element_type=F32
    )


def halves(re, im):
    return split(re), split(im), split(re + im)


def cdot(a, b):
    p1 = dot3(a[0], b[0])
    p2 = dot3(a[1], b[1])
    p3 = dot3(a[2], b[2])
    return p1 - p2, p3 - p1 - p2


def diagonal_mask():
    return lax.broadcasted_iota(jnp.int32, (N, N), 0) == lax.broadcasted_iota(jnp.int32, (N, N), 1)


def inverse(mr, mi):
    eye = diagonal_mask()

    def reciprocal(axis):
        dr = jnp.sum(jnp.where(eye, mr, 0.0), axis=axis, keepdims=True)
        di = jnp.sum(jnp.where(eye, mi, 0.0), axis=axis, keepdims=True)
        modulus = dr * dr + di * di
        return dr / modulus, -di / modulus

    xr, xi = reciprocal(0)
    rr = jnp.where(eye, 0.0, mi * xi - mr * xr)
    ri = jnp.where(eye, 0.0, -(mr * xi + mi * xr))
    r = halves(rr, ri)
    sr, si = cdot(r, r)
    s = halves(sr, si)
    tr, ti = cdot(s, s)
    ur, ui = cdot(r, s)
    yr = jnp.where(eye, 1.0, rr) + sr + ur
    yi = ri + si + ui
    ur, ui = cdot(halves(yr, yi), halves(tr, ti))
    yr = yr + ur
    yi = yi + ui
    cr, ci = reciprocal(1)
    return yr * cr - yi * ci, yr * ci + yi * cr


def couple(a, gr, gi, b):
    gr, gi = split(gr), split(gi)
    g = (cat([gr[0], gi[0]], 1), cat([gr[1], gi[1]], 1))
    hi, lo = split(dot3(a, g))
    hi = cat([hi[:, :N], hi[:, N:]], 0)
    lo = cat([lo[:, :N], lo[:, N:]], 0)
    both = dot3((hi, lo), b)
    return both[:N], both[N:]


def kernel(
    onsite, hop_in, coup_in, broad, born_in, shift, ploc_in, pside_in, out,
    hop, coup, born, ploc, pside, load,
    system, links, sig, green, late, hp, hm, ho, hf, wl, ws, ls, ss, sin, fcoup,
    chain_s, chain_r, y_s, y_r, o_s, o_r, f_s, f_r, side_s, side_r, pre_s, pre_r, go,
):
    e = lax.axis_index("energy")
    s = lax.axis_index("section")
    core = lax.rem(e, 2)
    other = e + 1 - 2 * core
    has_p = e < 30
    has_m = e >= 2
    has_right = s < 3
    has_left = s > 0
    middle = (s == 1) | (s == 2)
    early = jnp.where(s < 2, 1, 0)

    opening = jnp.where(s < 2, 0, 1)

    def loads(b):
        return [
            pltpu.make_async_copy(source.at[b], target.at[b], load.at[3 * b + k])
            for k, (source, target) in enumerate(((hop_in, hop), (born_in.at[0], born), (coup_in, coup)))
        ]

    def phonon_loads():
        return [
            pltpu.make_async_copy(ploc_in, ploc, load.at[6]),
            pltpu.make_async_copy(pside_in, pside, load.at[7]),
        ]

    for b in (opening, 1 - opening):
        for copy in loads(b):
            copy.start()
    for copy in phonon_loads():
        copy.start()

    barrier = pltpu.get_barrier_semaphore()

    def greet(cond, where):
        @pl.when(cond)
        def _():
            pl.semaphore_signal(barrier, inc=1, device_id=where, device_id_type=MESH)

    for distance in (1, 2, 3):
        pl.semaphore_signal(
            barrier, inc=1, device_id={"section": lax.rem(s + distance, 4)}, device_id_type=MESH
        )
    greet(has_p, {"energy": lax.rem(e + 2, 32)})
    greet(has_m, {"energy": lax.rem(e + 30, 32)})
    pl.semaphore_signal(barrier, inc=1, device_id={"energy": other}, device_id_type=MESH)

    def remote(src, dst, ssem, rsem, where):
        return pltpu.make_async_remote_copy(
            src_ref=src, dst_ref=dst, send_sem=ssem, recv_sem=rsem, device_id=where, device_id_type=MESH
        )

    def left_copy():
        return remote(sig.at[5], sig.at[1], chain_s.at[0], chain_r.at[0], {"section": lax.rem(s + 1, 4)})

    def right_copy():
        return remote(green.at[2], late.at[0], chain_s.at[1], chain_r.at[1], {"section": lax.rem(s + 3, 4)})

    def far_left_copy():
        return remote(sig.at[8], sig.at[1], chain_s.at[2], chain_r.at[0], {"section": lax.rem(s + 2, 4)})

    def far_right_copy():
        return remote(green.at[4], late.at[0], chain_s.at[2], chain_r.at[1], {"section": lax.rem(s + 2, 4)})

    swap = {"section": lax.rem(7 - s, 4)}

    def system_copy(b):
        return remote(system.at[b], system.at[2 + b], pre_s.at[b], pre_r.at[b], swap)

    def coupling_copy():
        return remote(coup, fcoup, pre_s.at[2], pre_r.at[2], swap)

    def y_copy(up, b, part):
        if up:
            return remote(green.at[b, part], hm.at[b, part], y_s.at[0, b, part], y_r.at[0, b, part],
                          {"energy": lax.rem(e + 2, 32)})
        return remote(green.at[b, part], hp.at[b, part], y_s.at[1, b, part], y_r.at[1, b, part],
                      {"energy": lax.rem(e + 30, 32)})

    def own_copy(b, part):
        return remote(green.at[b, part], ho.at[b, part], o_s.at[b, part], o_r.at[b, part], {"energy": other})

    def send_block(b):
        for part in range(UNITS):
            @pl.when(has_p)
            def _():
                y_copy(True, b, part).start()

            @pl.when(has_m)
            def _():
                y_copy(False, b, part).start()

    def fwd_copy(src, b, part):
        return remote(src.at[b, part], hf.at[b, part], f_s.at[b, part], f_r.at[b, part], {"energy": other})

    def side_right(part):
        return remote(ss.at[1, part], sin.at[0, part], side_s.at[1, part], side_r.at[0, part],
                      {"section": lax.rem(s + 1, 4)})

    def side_left(part):
        return remote(ss.at[0, part], sin.at[1, part], side_s.at[0, part], side_r.at[1, part],
                      {"section": lax.rem(s + 3, 4)})

    energy = -2.0 + 4.0 * e.astype(F32) / 31.0
    eta = broad[0]

    def link_halves(v, place):
        vh, vl = split(v)
        links[place, 0] = vh
        links[place, 1] = vl
        vh, vl = split(v.T)
        links[place, 2] = vh
        links[place, 3] = vl

    def setup(t, carry):
        b = opening + t - 2 * opening * t
        for copy in loads(b):
            copy.wait()
        eye = diagonal_mask()
        h = hop[b]
        ham = 0.5 * (h + h.T)
        system[b, 0] = jnp.where(eye, energy - onsite[pl.ds(b, 1), :], 0.0) - ham - born[b, 0]
        system[b, 1] = jnp.where(eye, eta, 0.0) - born[b, 1]
        link_halves(coup[b], b)
        return carry

    lax.fori_loop(0, 2, setup, 0)
    sig[0] = jnp.zeros((2, N, N), F32)

    @pl.when(s == 0)
    def _():
        sig[1] = jnp.zeros((2, N, N), F32)

    @pl.when(s == 3)
    def _():
        sig[4] = jnp.zeros((2, N, N), F32)

    def everyone_is_in():
        pl.semaphore_wait(barrier, 4 + has_p.astype(jnp.int32) + has_m.astype(jnp.int32))

    def weights():
        for copy in phonon_loads():
            copy.wait()

        def one(d, carry):
            wloc = jnp.zeros((N, N), F32)
            wside = jnp.zeros((N, N), F32)
            for k in range(MODES):
                on = jnp.where(shift[k] == d - 2, 1.0, 0.0)
                wloc = wloc + on * ploc[k]
                wside = wside + on * pside[k]
            wl[d] = wloc.reshape(CUTS, ROWS, N)
            ws[d] = wside.reshape(CUTS, ROWS, N)
            return carry

        lax.fori_loop(0, 5, one, 0)

    first_block = lax.rem(s, 2)
    last_block = 1 - first_block

    @pl.when(middle)
    def _():
        everyone_is_in()

    @pl.when(middle & (core == 0))
    def _():
        coupling_copy().start()
        system_copy(first_block).start()

    @pl.when(middle)
    def _():
        weights()

    @pl.when(middle & (core == 0))
    def _():
        coupling_copy().wait_recv()

        def foreign(b, carry):
            link_halves(fcoup[b], 2 + b)
            return carry

        lax.fori_loop(0, 2, foreign, 0)
        coupling_copy().wait_send()
        system_copy(last_block).start()

    def pick(b, values):
        return jnp.where(b == 0, values[0], jnp.where(b == 1, values[1], jnp.where(b == 2, values[2], values[3])))

    def slot(i, code):
        digit = lax.rem(code, 16)
        kind = digit // 4
        b = lax.rem(digit, 4)
        is_l = kind == 1
        is_r = kind == 2

        @pl.when((i == 2) & jnp.logical_not(middle))
        def _():
            weights()

        @pl.when(i == pick(s, (9, 0, 4 - 2 * core, 2)))
        def _():
            left_copy().wait_recv()

        @pl.when(i == pick(s, (2, 4 - 2 * core, 0, 9)))
        def _():
            right_copy().wait_recv()
            re, im = couple((links[1, 0], links[1, 1]), late[0, :CUTS].reshape(N, N), late[0, CUTS:].reshape(N, N), (links[1, 2], links[1, 3]))
            sig[4, 0] = re
            sig[4, 1] = im

        @pl.when(kind > 0)
        def _():
            @pl.when(b >= 2)
            def _():
                system_copy(b - 2).wait_recv()

            first = jnp.where(is_r, 0, pick(b, (1, 2, 5, 7)))
            second = jnp.where(is_l, 0, pick(b, (3, 4, 8, 7)))
            place = jnp.where(kind == 3, b, jnp.where(is_r, pick(b, (2, 3, 4, 3)), 3))
            re, im = inverse(
                system[b, 0] - sig[first, 0] - sig[second, 0], system[b, 1] - sig[first, 1] - sig[second, 1]
            )
            green[place, :CUTS] = re.reshape(CUTS, ROWS, N)
            green[place, CUTS:] = im.reshape(CUTS, ROWS, N)

            at_end = (i == 1) & jnp.logical_not(middle)

            @pl.when(at_end)
            def _():
                everyone_is_in()

            @pl.when(at_end & (s == 3) & (core == 1))
            def _():
                pl.semaphore_wait(go, 1)

            @pl.when(is_r & (b == 0))
            def _():
                right_copy().start()

            @pl.when(is_r & (b == 2))
            def _():
                far_right_copy().start()

            @pl.when(is_l | (is_r & ((b == 1) | (b == 3) | ((b == 0) & (s == 2) & (core == 0)))))
            def _():
                v = jnp.where(is_l, b, pick(b, (3, 0, 0, 2)))
                a0 = jnp.where(is_l, 2, 0)
                b0 = 2 - a0
                target = jnp.where(is_l, pick(b, (2, 5, 7, 8)), pick(b, (7, 3, 0, 8)))
                re, im = couple((links[v, a0], links[v, a0 + 1]), green[place, :CUTS].reshape(N, N), green[place, CUTS:].reshape(N, N),
                                (links[v, b0], links[v, b0 + 1]))
                sig[target, 0] = re
                sig[target, 1] = im

            @pl.when(at_end & (s == 0) & (core == 1))
            def _():
                pl.semaphore_wait(go, 1)

            @pl.when(is_l & (b == 1))
            def _():
                left_copy().start()

            @pl.when(is_l & (b == 3))
            def _():
                far_left_copy().start()

            @pl.when(at_end & (core == 0))
            def _():
                @pl.when(s == 0)
                def _():
                    left_copy().wait_send()

                @pl.when(s == 3)
                def _():
                    right_copy().wait_send()

                pl.semaphore_signal(go, inc=1, device_id={"energy": other}, device_id_type=MESH)

            @pl.when(kind == 3)
            def _():
                for part in range(UNITS):
                    own_copy(b, part).start()

                @pl.when(b == early)
                def _():
                    send_block(b)

        return code // 16

    codes = [pick(s, [order_code(x) for x in orders]) for orders in ORDERS]
    lax.fori_loop(0, SLOTS, slot, jnp.where(core == 0, codes[0], codes[1]))

    def units(t, carry):
        half = t // UNITS
        b = early + half - 2 * early * half
        part = lax.rem(t, UNITS)
        rows = lax.rem(t, CUTS)

        @pl.when(t == 0)
        def _():
            send_block(1 - early)

        def add(source, d):
            x = source[b, part]
            ls[b, part] = ls[b, part] + wl[d, rows] * x
            ss[b, part] = ss[b, part] + ws[d, rows] * x

        x = green[b, part]
        ls[b, part] = wl[2, rows] * x
        ss[b, part] = ws[2, rows] * x
        own_copy(b, part).wait_recv()
        add(ho, 3 - 2 * core)

        @pl.when(has_p)
        def _():
            y_copy(False, b, part).wait_recv()

            @pl.when(core == 0)
            def _():
                fwd_copy(hp, b, part).start()

            add(hp, 4)

        @pl.when(has_m)
        def _():
            y_copy(True, b, part).wait_recv()

            @pl.when(core == 1)
            def _():
                fwd_copy(hm, b, part).start()

            add(hm, 0)

        @pl.when(((core == 0) & has_m) | ((core == 1) & has_p))
        def _():
            fwd_copy(hp, b, part).wait_recv()
            add(hf, 1 + 2 * core)

        @pl.when((b == 1) & has_right)
        def _():
            side_right(part).start()

        @pl.when((b == 0) & has_left)
        def _():
            side_left(part).start()

        return carry

    lax.fori_loop(0, 2 * UNITS, units, 0)

    def finish(t, carry):
        b = t // UNITS
        part = lax.rem(t, UNITS)

        @pl.when((b == 0) & has_left)
        def _():
            side_right(part).wait_recv()

        @pl.when((b == 1) & has_right)
        def _():
            side_left(part).wait_recv()

        away = jnp.where(jnp.where(b == 0, has_left, has_right), sin[b, part], 0.0)
        rows = pl.ds(pl.multiple_of(lax.rem(t, CUTS) * ROWS, ROWS), ROWS)
        out[0, b, part // CUTS, rows, :] = ls[b, part] + ss[1 - b, part] + away
        return carry

    lax.fori_loop(0, 2 * UNITS, finish, 0)

    @pl.when(has_right)
    def _():
        for part in range(UNITS):
            side_right(part).wait_send()

        @pl.when((s == 1) | (core == 1))
        def _():
            left_copy().wait_send()

    @pl.when(has_left)
    def _():
        for part in range(UNITS):
            side_left(part).wait_send()

        @pl.when((s == 2) | (core == 1))
        def _():
            right_copy().wait_send()

    @pl.when(middle & (core == 0))
    def _():
        far_left_copy().wait_send()
        system_copy(first_block).wait_send()
        system_copy(last_block).wait_send()

    for b in range(2):
        for part in range(UNITS):
            own_copy(b, part).wait_send()

            @pl.when(has_p)
            def _():
                y_copy(True, b, part).wait_send()

            @pl.when(has_m)
            def _():
                y_copy(False, b, part).wait_send()

            @pl.when(((core == 0) & has_p) | ((core == 1) & has_m))
            def _():
                fwd_copy(hp, b, part).wait_send()


def local(onsite, hopping, coupling, broadening, born_sigma, phonon_shift, phonon_local, phonon_side):
    vmem = pl.BlockSpec(memory_space=pltpu.VMEM)
    smem = pl.BlockSpec(memory_space=pltpu.SMEM)
    hbm = pl.BlockSpec(memory_space=pl.ANY)
    dma = pltpu.SemaphoreType.DMA
    block = (2, N, N)
    pieces = (UNITS, ROWS, N)
    return pl.pallas_call(
        kernel,
        out_shape=pltpu.VMEM(born_sigma.shape, F32),
        in_specs=[vmem, hbm, hbm, smem, hbm, smem, hbm, hbm],
        out_specs=vmem,
        scratch_shapes=[
            pltpu.VMEM((2, N, N), F32),
            pltpu.VMEM((2, N, N), F32),
            pltpu.VMEM((2, 2, N, N), F32),
            pltpu.VMEM((MODES, N, N), F32),
            pltpu.VMEM((MODES, N, N), F32),
            dma((8,)),
            pltpu.VMEM((4,) + block, F32),
            pltpu.VMEM((4, 4, N, N), BF16),
            pltpu.VMEM((9,) + block, F32),
            pltpu.VMEM((5,) + pieces, F32),
            pltpu.VMEM((1,) + pieces, F32),
            pltpu.VMEM((2,) + pieces, F32),
            pltpu.VMEM((2,) + pieces, F32),
            pltpu.VMEM((2,) + pieces, F32),
            pltpu.VMEM((2,) + pieces, F32),
            pltpu.VMEM((5, CUTS, ROWS, N), F32),
            pltpu.VMEM((5, CUTS, ROWS, N), F32),
            pltpu.VMEM((2,) + pieces, F32),
            pltpu.VMEM((2,) + pieces, F32),
            pltpu.VMEM((2,) + pieces, F32),
            pltpu.VMEM(block, F32),
            dma((3,)), dma((2,)),
            dma((2, 2, UNITS)), dma((2, 2, UNITS)),
            dma((2, UNITS)), dma((2, UNITS)),
            dma((2, UNITS)), dma((2, UNITS)),
            dma((2, UNITS)), dma((2, UNITS)),
            dma((3,)), dma((3,)),
            pltpu.SemaphoreType.REGULAR,
        ],
        compiler_params=pltpu.CompilerParams(
            collective_id=0, has_side_effects=True, vmem_limit_bytes=56 * 2**20
        ),
        cost_estimate=pl.CostEstimate(flops=6 * 60 * 2 * N**3, bytes_accessed=6 * 2**20, transcendentals=0),
    )(onsite, hopping, coupling, broadening, born_sigma, phonon_shift, phonon_local, phonon_side)


def solution(mesh):
    in_specs = (
        P("section", None),
        P("section", None, None),
        P("section", None, None),
        P("energy"),
        P("energy", "section", None, None, None),
        P(),
        P(),
        P(),
    )
    out_specs = P("energy", "section", None, None, None)
    return jax.shard_map(local, mesh=mesh, in_specs=in_specs, out_specs=out_specs, check_vma=False)
```

```python
import jax
import jax.numpy as jnp
from jax import lax
from jax.experimental import pallas as pl
from jax.experimental.pallas import tpu as pltpu
from jax.sharding import PartitionSpec as P

MODES = 4
N = 256
F32 = jnp.float32
BF16 = jnp.bfloat16
MESH = pl.DeviceIdType.MESH

L, R, G = 4, 8, 12
ORDERS = (
    ((L, L + 1, G + 1, R + 1, G), (L, L + 1, L + 2, L + 3, G + 1, R + 1, G),
     (R + 1, R, R + 3, R + 2, G, L, G + 1), (R + 1, R, G, L, G + 1)),
    ((L, L + 1, G + 1, R + 1, G), (L, L + 1, R + 1, R, G + 1, G),
     (R + 1, R, L, L + 1, G, G + 1), (R + 1, R, G, L, G + 1)),
)
SLOTS = 7
CUTS = 2
UNITS = 2 * CUTS
ROWS = N // CUTS


def order_code(steps):
    return sum(step * 16**i for i, step in enumerate(steps))


def cat(parts, axis):
    return jnp.concatenate(parts, axis=axis)


def split(x):
    hi = x.astype(BF16)
    return hi, (x - hi.astype(F32)).astype(BF16)


def dot3(a, b):
    return jnp.dot(
        cat([a[0], a[1], a[0]], 1), cat([b[0], b[0], b[1]], 0), preferred_element_type=F32
    )


def halves(re, im):
    return split(re), split(im), split(re + im)


def cdot(a, b):
    p1 = dot3(a[0], b[0])
    p2 = dot3(a[1], b[1])
    p3 = dot3(a[2], b[2])
    return p1 - p2, p3 - p1 - p2


def diagonal_mask():
    return lax.broadcasted_iota(jnp.int32, (N, N), 0) == lax.broadcasted_iota(jnp.int32, (N, N), 1)


def inverse(mr, mi):
    eye = diagonal_mask()

    def reciprocal(axis):
        dr = jnp.sum(jnp.where(eye, mr, 0.0), axis=axis, keepdims=True)
        di = jnp.sum(jnp.where(eye, mi, 0.0), axis=axis, keepdims=True)
        modulus = dr * dr + di * di
        return dr / modulus, -di / modulus

    xr, xi = reciprocal(0)
    rr = jnp.where(eye, 0.0, mi * xi - mr * xr)
    ri = jnp.where(eye, 0.0, -(mr * xi + mi * xr))
    r = halves(rr, ri)
    sr, si = cdot(r, r)
    s = halves(sr, si)
    tr, ti = cdot(s, s)
    ur, ui = cdot(r, s)
    yr = jnp.where(eye, 1.0, rr) + sr + ur
    yi = ri + si + ui
    ur, ui = cdot(halves(yr, yi), halves(tr, ti))
    yr = yr + ur
    yi = yi + ui
    cr, ci = reciprocal(1)
    return yr * cr - yi * ci, yr * ci + yi * cr


def couple(a, gr, gi, b):
    gr, gi = split(gr), split(gi)
    g = (cat([gr[0], gi[0]], 1), cat([gr[1], gi[1]], 1))
    hi, lo = split(dot3(a, g))
    hi = cat([hi[:, :N], hi[:, N:]], 0)
    lo = cat([lo[:, :N], lo[:, N:]], 0)
    both = dot3((hi, lo), b)
    return both[:N], both[N:]


def kernel(
    onsite, hop_in, coup_in, broad, born_in, shift, ploc_in, pside_in, out,
    hop, coup, born, ploc, pside, load,
    system, links, sig, green, late, hp, hm, ho, hf, wl, ws, ls, ss, sin, fcoup,
    chain_s, chain_r, y_s, y_r, o_s, o_r, f_s, f_r, side_s, side_r, pre_s, pre_r, go,
):
    e = lax.axis_index("energy")
    s = lax.axis_index("section")
    core = lax.rem(e, 2)
    other = e + 1 - 2 * core
    has_p = e < 30
    has_m = e >= 2
    has_right = s < 3
    has_left = s > 0
    middle = (s == 1) | (s == 2)
    early = jnp.where(s < 2, 1, 0)

    opening = jnp.where(s < 2, 0, 1)

    def loads(b):
        return [
            pltpu.make_async_copy(source.at[b], target.at[b], load.at[3 * b + k])
            for k, (source, target) in enumerate(((hop_in, hop), (born_in.at[0], born), (coup_in, coup)))
        ]

    def phonon_loads():
        return [
            pltpu.make_async_copy(ploc_in, ploc, load.at[6]),
            pltpu.make_async_copy(pside_in, pside, load.at[7]),
        ]

    for b in (opening, 1 - opening):
        for copy in loads(b):
            copy.start()
    for copy in phonon_loads():
        copy.start()

    barrier = pltpu.get_barrier_semaphore()

    def greet(cond, where):
        @pl.when(cond)
        def _():
            pl.semaphore_signal(barrier, inc=1, device_id=where, device_id_type=MESH)

    for distance in (1, 2, 3):
        pl.semaphore_signal(
            barrier, inc=1, device_id={"section": lax.rem(s + distance, 4)}, device_id_type=MESH
        )
    greet(has_p, {"energy": lax.rem(e + 2, 32)})
    greet(has_m, {"energy": lax.rem(e + 30, 32)})
    pl.semaphore_signal(barrier, inc=1, device_id={"energy": other}, device_id_type=MESH)

    def remote(src, dst, ssem, rsem, where):
        return pltpu.make_async_remote_copy(
            src_ref=src, dst_ref=dst, send_sem=ssem, recv_sem=rsem, device_id=where, device_id_type=MESH
        )

    def left_copy():
        return remote(sig.at[5], sig.at[1], chain_s.at[0], chain_r.at[0], {"section": lax.rem(s + 1, 4)})

    def right_copy():
        return remote(green.at[2], late.at[0], chain_s.at[1], chain_r.at[1], {"section": lax.rem(s + 3, 4)})

    def far_left_copy():
        return remote(sig.at[8], sig.at[1], chain_s.at[2], chain_r.at[0], {"section": lax.rem(s + 2, 4)})

    def far_right_copy():
        return remote(green.at[4], late.at[0], chain_s.at[2], chain_r.at[1], {"section": lax.rem(s + 2, 4)})

    swap = {"section": lax.rem(7 - s, 4)}

    def system_copy(b):
        return remote(system.at[b], system.at[2 + b], pre_s.at[b], pre_r.at[b], swap)

    def coupling_copy():
        return remote(coup, fcoup, pre_s.at[2], pre_r.at[2], swap)

    def y_copy(up, b, part):
        if up:
            return remote(green.at[b, part], hm.at[b, part], y_s.at[0, b, part], y_r.at[0, b, part],
                          {"energy": lax.rem(e + 2, 32)})
        return remote(green.at[b, part], hp.at[b, part], y_s.at[1, b, part], y_r.at[1, b, part],
                      {"energy": lax.rem(e + 30, 32)})

    def own_copy(b, part):
        return remote(green.at[b, part], ho.at[b, part], o_s.at[b, part], o_r.at[b, part], {"energy": other})

    def send_block(b):
        for part in range(UNITS):
            @pl.when(has_p)
            def _():
                y_copy(True, b, part).start()

            @pl.when(has_m)
            def _():
                y_copy(False, b, part).start()

    def fwd_copy(src, b, part):
        return remote(src.at[b, part], hf.at[b, part], f_s.at[b, part], f_r.at[b, part], {"energy": other})

    def side_right(part):
        return remote(ss.at[1, part], sin.at[0, part], side_s.at[1, part], side_r.at[0, part],
                      {"section": lax.rem(s + 1, 4)})

    def side_left(part):
        return remote(ss.at[0, part], sin.at[1, part], side_s.at[0, part], side_r.at[1, part],
                      {"section": lax.rem(s + 3, 4)})

    energy = -2.0 + 4.0 * e.astype(F32) / 31.0
    eta = broad[0]

    def link_halves(v, place):
        vh, vl = split(v)
        links[place, 0] = vh
        links[place, 1] = vl
        vh, vl = split(v.T)
        links[place, 2] = vh
        links[place, 3] = vl

    def setup(t, carry):
        b = opening + t - 2 * opening * t
        for copy in loads(b):
            copy.wait()
        eye = diagonal_mask()
        h = hop[b]
        ham = 0.5 * (h + h.T)
        system[b, 0] = jnp.where(eye, energy - onsite[pl.ds(b, 1), :], 0.0) - ham - born[b, 0]
        system[b, 1] = jnp.where(eye, eta, 0.0) - born[b, 1]
        link_halves(coup[b], b)
        return carry

    lax.fori_loop(0, 2, setup, 0)
    sig[0] = jnp.zeros((2, N, N), F32)

    @pl.when(s == 0)
    def _():
        sig[1] = jnp.zeros((2, N, N), F32)

    @pl.when(s == 3)
    def _():
        sig[4] = jnp.zeros((2, N, N), F32)

    def everyone_is_in():
        pl.semaphore_wait(barrier, 4 + has_p.astype(jnp.int32) + has_m.astype(jnp.int32))

    def weights():
        for copy in phonon_loads():
            copy.wait()

        def one(d, carry):
            wloc = jnp.zeros((N, N), F32)
            wside = jnp.zeros((N, N), F32)
            for k in range(MODES):
                on = jnp.where(shift[k] == d - 2, 1.0, 0.0)
                wloc = wloc + on * ploc[k]
                wside = wside + on * pside[k]
            wl[d] = wloc.reshape(CUTS, ROWS, N)
            ws[d] = wside.reshape(CUTS, ROWS, N)
            return carry

        lax.fori_loop(0, 5, one, 0)

    first_block = lax.rem(s, 2)
    last_block = 1 - first_block

    @pl.when(middle)
    def _():
        everyone_is_in()

    @pl.when(middle & (core == 0))
    def _():
        coupling_copy().start()
        system_copy(first_block).start()

    @pl.when(middle)
    def _():
        weights()

    @pl.when(middle & (core == 0))
    def _():
        coupling_copy().wait_recv()

        def foreign(b, carry):
            link_halves(fcoup[b], 2 + b)
            return carry

        lax.fori_loop(0, 2, foreign, 0)
        coupling_copy().wait_send()
        system_copy(last_block).start()

    def pick(b, values):
        return jnp.where(b == 0, values[0], jnp.where(b == 1, values[1], jnp.where(b == 2, values[2], values[3])))

    def slot(i, code):
        digit = lax.rem(code, 16)
        kind = digit // 4
        b = lax.rem(digit, 4)
        is_l = kind == 1
        is_r = kind == 2

        @pl.when((i == 2) & jnp.logical_not(middle))
        def _():
            weights()

        @pl.when(i == pick(s, (9, 0, 4 - 2 * core, 2)))
        def _():
            left_copy().wait_recv()

        @pl.when(i == pick(s, (2, 4 - 2 * core, 0, 9)))
        def _():
            right_copy().wait_recv()
            re, im = couple((links[1, 0], links[1, 1]), late[0, :CUTS].reshape(N, N), late[0, CUTS:].reshape(N, N), (links[1, 2], links[1, 3]))
            sig[4, 0] = re
            sig[4, 1] = im

        @pl.when(kind > 0)
        def _():
            @pl.when(b >= 2)
            def _():
                system_copy(b - 2).wait_recv()

            first = jnp.where(is_r, 0, pick(b, (1, 2, 5, 7)))
            second = jnp.where(is_l, 0, pick(b, (3, 4, 8, 7)))
            place = jnp.where(kind == 3, b, jnp.where(is_r, pick(b, (2, 3, 4, 3)), 3))
            re, im = inverse(
                system[b, 0] - sig[first, 0] - sig[second, 0], system[b, 1] - sig[first, 1] - sig[second, 1]
            )
            green[place, :CUTS] = re.reshape(CUTS, ROWS, N)
            green[place, CUTS:] = im.reshape(CUTS, ROWS, N)

            at_end = (i == 1) & jnp.logical_not(middle)

            @pl.when(at_end)
            def _():
                everyone_is_in()

            @pl.when(at_end & (s == 3) & (core == 1))
            def _():
                pl.semaphore_wait(go, 1)

            @pl.when(is_r & (b == 0))
            def _():
                right_copy().start()

            @pl.when(is_r & (b == 2))
            def _():
                far_right_copy().start()

            @pl.when(is_l | (is_r & ((b == 1) | (b == 3) | ((b == 0) & (s == 2) & (core == 0)))))
            def _():
                v = jnp.where(is_l, b, pick(b, (3, 0, 0, 2)))
                a0 = jnp.where(is_l, 2, 0)
                b0 = 2 - a0
                target = jnp.where(is_l, pick(b, (2, 5, 7, 8)), pick(b, (7, 3, 0, 8)))
                re, im = couple((links[v, a0], links[v, a0 + 1]), green[place, :CUTS].reshape(N, N), green[place, CUTS:].reshape(N, N),
                                (links[v, b0], links[v, b0 + 1]))
                sig[target, 0] = re
                sig[target, 1] = im

            @pl.when(at_end & (s == 0) & (core == 1))
            def _():
                pl.semaphore_wait(go, 1)

            @pl.when(is_l & (b == 1))
            def _():
                left_copy().start()

            @pl.when(is_l & (b == 3))
            def _():
                far_left_copy().start()

            @pl.when(at_end & (core == 0))
            def _():
                @pl.when(s == 0)
                def _():
                    left_copy().wait_send()

                @pl.when(s == 3)
                def _():
                    right_copy().wait_send()

                pl.semaphore_signal(go, inc=1, device_id={"energy": other}, device_id_type=MESH)

            @pl.when(kind == 3)
            def _():
                for part in range(UNITS):
                    own_copy(b, part).start()

                @pl.when(b == early)
                def _():
                    send_block(b)

        return code // 16

    codes = [pick(s, [order_code(x) for x in orders]) for orders in ORDERS]
    lax.fori_loop(0, SLOTS, slot, jnp.where(core == 0, codes[0], codes[1]))

    def units(t, carry):
        half = t // UNITS
        b = early + half - 2 * early * half
        part = lax.rem(t, UNITS)
        rows = lax.rem(t, CUTS)

        @pl.when(t == 0)
        def _():
            send_block(1 - early)

        @pl.when(has_p)
        def _():
            y_copy(False, b, part).wait_recv()

            @pl.when(core == 0)
            def _():
                fwd_copy(hp, b, part).start()

        @pl.when(has_m)
        def _():
            y_copy(True, b, part).wait_recv()

            @pl.when(core == 1)
            def _():
                fwd_copy(hm, b, part).start()

        own_copy(b, part).wait_recv()
        x = green[b, part]
        near = ho[b, part]
        up = jnp.where(has_p, hp[b, part], 0.0)
        down = jnp.where(has_m, hm[b, part], 0.0)
        d = 3 - 2 * core
        ls[b, part] = wl[2, rows] * x + wl[d, rows] * near + wl[4, rows] * up + wl[0, rows] * down
        ss[b, part] = ws[2, rows] * x + ws[d, rows] * near + ws[4, rows] * up + ws[0, rows] * down

        @pl.when(((core == 0) & has_m) | ((core == 1) & has_p))
        def _():
            fwd_copy(hp, b, part).wait_recv()
            x = hf[b, part]
            d = 1 + 2 * core
            ss[b, part] = ss[b, part] + ws[d, rows] * x
            ls[b, part] = ls[b, part] + wl[d, rows] * x

        @pl.when((b == 1) & has_right)
        def _():
            side_right(part).start()

        @pl.when((b == 0) & has_left)
        def _():
            side_left(part).start()

        return carry

    lax.fori_loop(0, 2 * UNITS, units, 0)

    def finish(t, carry):
        b = t // UNITS
        part = lax.rem(t, UNITS)

        @pl.when((b == 0) & has_left)
        def _():
            side_right(part).wait_recv()

        @pl.when((b == 1) & has_right)
        def _():
            side_left(part).wait_recv()

        away = jnp.where(jnp.where(b == 0, has_left, has_right), sin[b, part], 0.0)
        rows = pl.ds(pl.multiple_of(lax.rem(t, CUTS) * ROWS, ROWS), ROWS)
        out[0, b, part // CUTS, rows, :] = ls[b, part] + ss[1 - b, part] + away
        return carry

    lax.fori_loop(0, 2 * UNITS, finish, 0)

    @pl.when(has_right)
    def _():
        for part in range(UNITS):
            side_right(part).wait_send()

        @pl.when((s == 1) | (core == 1))
        def _():
            left_copy().wait_send()

    @pl.when(has_left)
    def _():
        for part in range(UNITS):
            side_left(part).wait_send()

        @pl.when((s == 2) | (core == 1))
        def _():
            right_copy().wait_send()

    @pl.when(middle & (core == 0))
    def _():
        far_left_copy().wait_send()
        system_copy(first_block).wait_send()
        system_copy(last_block).wait_send()

    for b in range(2):
        for part in range(UNITS):
            own_copy(b, part).wait_send()

            @pl.when(has_p)
            def _():
                y_copy(True, b, part).wait_send()

            @pl.when(has_m)
            def _():
                y_copy(False, b, part).wait_send()

            @pl.when(((core == 0) & has_p) | ((core == 1) & has_m))
            def _():
                fwd_copy(hp, b, part).wait_send()


def local(onsite, hopping, coupling, broadening, born_sigma, phonon_shift, phonon_local, phonon_side):
    vmem = pl.BlockSpec(memory_space=pltpu.VMEM)
    smem = pl.BlockSpec(memory_space=pltpu.SMEM)
    hbm = pl.BlockSpec(memory_space=pl.ANY)
    dma = pltpu.SemaphoreType.DMA
    block = (2, N, N)
    pieces = (UNITS, ROWS, N)
    return pl.pallas_call(
        kernel,
        out_shape=pltpu.VMEM(born_sigma.shape, F32),
        in_specs=[vmem, hbm, hbm, smem, hbm, smem, hbm, hbm],
        out_specs=vmem,
        scratch_shapes=[
            pltpu.VMEM((2, N, N), F32),
            pltpu.VMEM((2, N, N), F32),
            pltpu.VMEM((2, 2, N, N), F32),
            pltpu.VMEM((MODES, N, N), F32),
            pltpu.VMEM((MODES, N, N), F32),
            dma((8,)),
            pltpu.VMEM((4,) + block, F32),
            pltpu.VMEM((4, 4, N, N), BF16),
            pltpu.VMEM((9,) + block, F32),
            pltpu.VMEM((5,) + pieces, F32),
            pltpu.VMEM((1,) + pieces, F32),
            pltpu.VMEM((2,) + pieces, F32),
            pltpu.VMEM((2,) + pieces, F32),
            pltpu.VMEM((2,) + pieces, F32),
            pltpu.VMEM((2,) + pieces, F32),
            pltpu.VMEM((5, CUTS, ROWS, N), F32),
            pltpu.VMEM((5, CUTS, ROWS, N), F32),
            pltpu.VMEM((2,) + pieces, F32),
            pltpu.VMEM((2,) + pieces, F32),
            pltpu.VMEM((2,) + pieces, F32),
            pltpu.VMEM(block, F32),
            dma((3,)), dma((2,)),
            dma((2, 2, UNITS)), dma((2, 2, UNITS)),
            dma((2, UNITS)), dma((2, UNITS)),
            dma((2, UNITS)), dma((2, UNITS)),
            dma((2, UNITS)), dma((2, UNITS)),
            dma((3,)), dma((3,)),
            pltpu.SemaphoreType.REGULAR,
        ],
        compiler_params=pltpu.CompilerParams(
            collective_id=0, has_side_effects=True, vmem_limit_bytes=56 * 2**20
        ),
        cost_estimate=pl.CostEstimate(flops=6 * 60 * 2 * N**3, bytes_accessed=6 * 2**20, transcendentals=0),
    )(onsite, hopping, coupling, broadening, born_sigma, phonon_shift, phonon_local, phonon_side)


def solution(mesh):
    in_specs = (
        P("section", None),
        P("section", None, None),
        P("section", None, None),
        P("energy"),
        P("energy", "section", None, None, None),
        P(),
        P(),
        P(),
    )
    out_specs = P("energy", "section", None, None, None)
    return jax.shard_map(local, mesh=mesh, in_specs=in_specs, out_specs=out_specs, check_vma=False)
```

```python
import jax
import jax.numpy as jnp
from jax import lax
from jax.experimental import pallas as pl
from jax.experimental.pallas import tpu as pltpu
from jax.sharding import PartitionSpec as P

MODES = 4
N = 256
F32 = jnp.float32
BF16 = jnp.bfloat16
MESH = pl.DeviceIdType.MESH

L, R, G = 4, 8, 12
ORDERS = (
    ((L, L + 1, G + 1, R + 1, G), (L, L + 1, L + 2, L + 3, G + 1, R + 1, G),
     (R + 1, R, R + 3, R + 2, G, L, G + 1), (R + 1, R, G, L, G + 1)),
    ((L, L + 1, G + 1, R + 1, G), (L, L + 1, R + 1, R, G + 1, G),
     (R + 1, R, L, L + 1, G, G + 1), (R + 1, R, G, L, G + 1)),
)
SLOTS = 7
CUTS = 2
UNITS = 2 * CUTS
ROWS = N // CUTS


def order_code(steps):
    return sum(step * 16**i for i, step in enumerate(steps))


def cat(parts, axis):
    return jnp.concatenate(parts, axis=axis)


def split(x):
    hi = x.astype(BF16)
    return hi, (x - hi.astype(F32)).astype(BF16)


def dot3(a, b):
    def dot(x, y):
        return jnp.dot(x, y, preferred_element_type=F32)

    return dot(a[0], b[0]) + dot(a[1], b[0]) + dot(a[0], b[1])


def halves(re, im):
    return split(re), split(im), split(re + im)


def cdot(a, b):
    p1 = dot3(a[0], b[0])
    p2 = dot3(a[1], b[1])
    p3 = dot3(a[2], b[2])
    return p1 - p2, p3 - p1 - p2


def diagonal_mask():
    return lax.broadcasted_iota(jnp.int32, (N, N), 0) == lax.broadcasted_iota(jnp.int32, (N, N), 1)


def inverse(mr, mi):
    eye = diagonal_mask()

    def reciprocal(axis):
        dr = jnp.sum(jnp.where(eye, mr, 0.0), axis=axis, keepdims=True)
        di = jnp.sum(jnp.where(eye, mi, 0.0), axis=axis, keepdims=True)
        modulus = dr * dr + di * di
        return dr / modulus, -di / modulus

    xr, xi = reciprocal(0)
    rr = jnp.where(eye, 0.0, mi * xi - mr * xr)
    ri = jnp.where(eye, 0.0, -(mr * xi + mi * xr))
    r = halves(rr, ri)
    sr, si = cdot(r, r)
    s = halves(sr, si)
    tr, ti = cdot(s, s)
    ur, ui = cdot(r, s)
    yr = jnp.where(eye, 1.0, rr) + sr + ur
    yi = ri + si + ui
    ur, ui = cdot(halves(yr, yi), halves(tr, ti))
    yr = yr + ur
    yi = yi + ui
    cr, ci = reciprocal(1)
    return yr * cr - yi * ci, yr * ci + yi * cr


def couple(a, gr, gi, b):
    gr, gi = split(gr), split(gi)
    g = (cat([gr[0], gi[0]], 1), cat([gr[1], gi[1]], 1))
    hi, lo = split(dot3(a, g))
    hi = cat([hi[:, :N], hi[:, N:]], 0)
    lo = cat([lo[:, :N], lo[:, N:]], 0)
    both = dot3((hi, lo), b)
    return both[:N], both[N:]


def kernel(
    onsite, hop_in, coup_in, broad, born_in, shift, ploc_in, pside_in, out,
    hop, coup, born, ploc, pside, load,
    system, links, sig, green, late, hp, hm, ho, hf, wl, ws, ls, ss, sin, fcoup,
    chain_s, chain_r, y_s, y_r, o_s, o_r, f_s, f_r, side_s, side_r, pre_s, pre_r, go,
):
    e = lax.axis_index("energy")
    s = lax.axis_index("section")
    core = lax.rem(e, 2)
    other = e + 1 - 2 * core
    has_p = e < 30
    has_m = e >= 2
    has_right = s < 3
    has_left = s > 0
    middle = (s == 1) | (s == 2)
    early = jnp.where(s < 2, 1, 0)

    opening = jnp.where(s < 2, 0, 1)

    def loads(b):
        return [
            pltpu.make_async_copy(source.at[b], target.at[b], load.at[3 * b + k])
            for k, (source, target) in enumerate(((hop_in, hop), (born_in.at[0], born), (coup_in, coup)))
        ]

    def phonon_loads():
        return [
            pltpu.make_async_copy(ploc_in, ploc, load.at[6]),
            pltpu.make_async_copy(pside_in, pside, load.at[7]),
        ]

    for b in (opening, 1 - opening):
        for copy in loads(b):
            copy.start()
    for copy in phonon_loads():
        copy.start()

    barrier = pltpu.get_barrier_semaphore()

    def greet(cond, where):
        @pl.when(cond)
        def _():
            pl.semaphore_signal(barrier, inc=1, device_id=where, device_id_type=MESH)

    for distance in (1, 2, 3):
        pl.semaphore_signal(
            barrier, inc=1, device_id={"section": lax.rem(s + distance, 4)}, device_id_type=MESH
        )
    greet(has_p, {"energy": lax.rem(e + 2, 32)})
    greet(has_m, {"energy": lax.rem(e + 30, 32)})
    pl.semaphore_signal(barrier, inc=1, device_id={"energy": other}, device_id_type=MESH)

    def remote(src, dst, ssem, rsem, where):
        return pltpu.make_async_remote_copy(
            src_ref=src, dst_ref=dst, send_sem=ssem, recv_sem=rsem, device_id=where, device_id_type=MESH
        )

    def left_copy():
        return remote(sig.at[5], sig.at[1], chain_s.at[0], chain_r.at[0], {"section": lax.rem(s + 1, 4)})

    def right_copy():
        return remote(green.at[2], late.at[0], chain_s.at[1], chain_r.at[1], {"section": lax.rem(s + 3, 4)})

    def far_left_copy():
        return remote(sig.at[8], sig.at[1], chain_s.at[2], chain_r.at[0], {"section": lax.rem(s + 2, 4)})

    def far_right_copy():
        return remote(green.at[4], late.at[0], chain_s.at[2], chain_r.at[1], {"section": lax.rem(s + 2, 4)})

    swap = {"section": lax.rem(7 - s, 4)}

    def system_copy(b):
        return remote(system.at[b], system.at[2 + b], pre_s.at[b], pre_r.at[b], swap)

    def coupling_copy():
        return remote(coup, fcoup, pre_s.at[2], pre_r.at[2], swap)

    def y_copy(up, b, part):
        if up:
            return remote(green.at[b, part], hm.at[b, part], y_s.at[0, b, part], y_r.at[0, b, part],
                          {"energy": lax.rem(e + 2, 32)})
        return remote(green.at[b, part], hp.at[b, part], y_s.at[1, b, part], y_r.at[1, b, part],
                      {"energy": lax.rem(e + 30, 32)})

    def own_copy(b, part):
        return remote(green.at[b, part], ho.at[b, part], o_s.at[b, part], o_r.at[b, part], {"energy": other})

    def send_block(b):
        for part in range(UNITS):
            @pl.when(has_p)
            def _():
                y_copy(True, b, part).start()

            @pl.when(has_m)
            def _():
                y_copy(False, b, part).start()

    def fwd_copy(src, b, part):
        return remote(src.at[b, part], hf.at[b, part], f_s.at[b, part], f_r.at[b, part], {"energy": other})

    def side_right(part):
        return remote(ss.at[1, part], sin.at[0, part], side_s.at[1, part], side_r.at[0, part],
                      {"section": lax.rem(s + 1, 4)})

    def side_left(part):
        return remote(ss.at[0, part], sin.at[1, part], side_s.at[0, part], side_r.at[1, part],
                      {"section": lax.rem(s + 3, 4)})

    energy = -2.0 + 4.0 * e.astype(F32) / 31.0
    eta = broad[0]

    def link_halves(v, place):
        vh, vl = split(v)
        links[place, 0] = vh
        links[place, 1] = vl
        vh, vl = split(v.T)
        links[place, 2] = vh
        links[place, 3] = vl

    def setup(t, carry):
        b = opening + t - 2 * opening * t
        for copy in loads(b):
            copy.wait()
        eye = diagonal_mask()
        h = hop[b]
        ham = 0.5 * (h + h.T)
        system[b, 0] = jnp.where(eye, energy - onsite[pl.ds(b, 1), :], 0.0) - ham - born[b, 0]
        system[b, 1] = jnp.where(eye, eta, 0.0) - born[b, 1]
        link_halves(coup[b], b)
        return carry

    lax.fori_loop(0, 2, setup, 0)
    sig[0] = jnp.zeros((2, N, N), F32)

    @pl.when(s == 0)
    def _():
        sig[1] = jnp.zeros((2, N, N), F32)

    @pl.when(s == 3)
    def _():
        sig[4] = jnp.zeros((2, N, N), F32)

    def everyone_is_in():
        pl.semaphore_wait(barrier, 4 + has_p.astype(jnp.int32) + has_m.astype(jnp.int32))

    def weights():
        for copy in phonon_loads():
            copy.wait()

        def one(d, carry):
            wloc = jnp.zeros((N, N), F32)
            wside = jnp.zeros((N, N), F32)
            for k in range(MODES):
                on = jnp.where(shift[k] == d - 2, 1.0, 0.0)
                wloc = wloc + on * ploc[k]
                wside = wside + on * pside[k]
            wl[d] = wloc.reshape(CUTS, ROWS, N)
            ws[d] = wside.reshape(CUTS, ROWS, N)
            return carry

        lax.fori_loop(0, 5, one, 0)

    first_block = lax.rem(s, 2)
    last_block = 1 - first_block

    @pl.when(middle)
    def _():
        everyone_is_in()

    @pl.when(middle & (core == 0))
    def _():
        coupling_copy().start()
        system_copy(first_block).start()

    @pl.when(middle)
    def _():
        weights()

    @pl.when(middle & (core == 0))
    def _():
        coupling_copy().wait_recv()

        def foreign(b, carry):
            link_halves(fcoup[b], 2 + b)
            return carry

        lax.fori_loop(0, 2, foreign, 0)
        coupling_copy().wait_send()
        system_copy(last_block).start()

    def pick(b, values):
        return jnp.where(b == 0, values[0], jnp.where(b == 1, values[1], jnp.where(b == 2, values[2], values[3])))

    def slot(i, code):
        digit = lax.rem(code, 16)
        kind = digit // 4
        b = lax.rem(digit, 4)
        is_l = kind == 1
        is_r = kind == 2

        @pl.when((i == 2) & jnp.logical_not(middle))
        def _():
            weights()

        @pl.when(i == pick(s, (9, 0, 4 - 2 * core, 2)))
        def _():
            left_copy().wait_recv()

        @pl.when(i == pick(s, (2, 4 - 2 * core, 0, 9)))
        def _():
            right_copy().wait_recv()
            re, im = couple((links[1, 0], links[1, 1]), late[0, :CUTS].reshape(N, N), late[0, CUTS:].reshape(N, N), (links[1, 2], links[1, 3]))
            sig[4, 0] = re
            sig[4, 1] = im

        @pl.when(kind > 0)
        def _():
            @pl.when(b >= 2)
            def _():
                system_copy(b - 2).wait_recv()

            first = jnp.where(is_r, 0, pick(b, (1, 2, 5, 7)))
            second = jnp.where(is_l, 0, pick(b, (3, 4, 8, 7)))
            place = jnp.where(kind == 3, b, jnp.where(is_r, pick(b, (2, 3, 4, 3)), 3))
            re, im = inverse(
                system[b, 0] - sig[first, 0] - sig[second, 0], system[b, 1] - sig[first, 1] - sig[second, 1]
            )
            green[place, :CUTS] = re.reshape(CUTS, ROWS, N)
            green[place, CUTS:] = im.reshape(CUTS, ROWS, N)

            at_end = (i == 1) & jnp.logical_not(middle)

            @pl.when(at_end)
            def _():
                everyone_is_in()

            @pl.when(at_end & (s == 3) & (core == 1))
            def _():
                pl.semaphore_wait(go, 1)

            held_back = middle & (core == 0)

            @pl.when(is_r & (b == 0) & jnp.logical_not(held_back))
            def _():
                right_copy().start()

            @pl.when(held_back & (i == 2) & (s == 2))
            def _():
                right_copy().start()

            @pl.when(held_back & (i == 2) & (s == 1))
            def _():
                left_copy().start()

            @pl.when(is_r & (b == 2))
            def _():
                far_right_copy().start()

            @pl.when(is_l | (is_r & ((b == 1) | (b == 3) | ((b == 0) & (s == 2) & (core == 0)))))
            def _():
                v = jnp.where(is_l, b, pick(b, (3, 0, 0, 2)))
                a0 = jnp.where(is_l, 2, 0)
                b0 = 2 - a0
                target = jnp.where(is_l, pick(b, (2, 5, 7, 8)), pick(b, (7, 3, 0, 8)))
                re, im = couple((links[v, a0], links[v, a0 + 1]), green[place, :CUTS].reshape(N, N), green[place, CUTS:].reshape(N, N),
                                (links[v, b0], links[v, b0 + 1]))
                sig[target, 0] = re
                sig[target, 1] = im

            @pl.when(at_end & (s == 0) & (core == 1))
            def _():
                pl.semaphore_wait(go, 1)

            @pl.when(is_l & (b == 1) & jnp.logical_not(held_back))
            def _():
                left_copy().start()

            @pl.when(is_l & (b == 3))
            def _():
                far_left_copy().start()

            @pl.when(at_end & (core == 0))
            def _():
                @pl.when(s == 0)
                def _():
                    left_copy().wait_send()

                @pl.when(s == 3)
                def _():
                    right_copy().wait_send()

                pl.semaphore_signal(go, inc=1, device_id={"energy": other}, device_id_type=MESH)

            @pl.when(kind == 3)
            def _():
                for part in range(UNITS):
                    own_copy(b, part).start()

                @pl.when(b == early)
                def _():
                    send_block(b)

        return code // 16

    codes = [pick(s, [order_code(x) for x in orders]) for orders in ORDERS]
    lax.fori_loop(0, SLOTS, slot, jnp.where(core == 0, codes[0], codes[1]))

    def units(t, carry):
        half = t // UNITS
        b = early + half - 2 * early * half
        part = lax.rem(t, UNITS)
        rows = lax.rem(t, CUTS)

        @pl.when(t == 0)
        def _():
            send_block(1 - early)

        @pl.when(has_p)
        def _():
            y_copy(False, b, part).wait_recv()

            @pl.when(core == 0)
            def _():
                fwd_copy(hp, b, part).start()

        @pl.when(has_m)
        def _():
            y_copy(True, b, part).wait_recv()

            @pl.when(core == 1)
            def _():
                fwd_copy(hm, b, part).start()

        own_copy(b, part).wait_recv()
        x = green[b, part]
        near = ho[b, part]
        up = jnp.where(has_p, hp[b, part], 0.0)
        down = jnp.where(has_m, hm[b, part], 0.0)
        d = 3 - 2 * core
        ls[b, part] = wl[2, rows] * x + wl[d, rows] * near + wl[4, rows] * up + wl[0, rows] * down
        ss[b, part] = ws[2, rows] * x + ws[d, rows] * near + ws[4, rows] * up + ws[0, rows] * down

        @pl.when(((core == 0) & has_m) | ((core == 1) & has_p))
        def _():
            fwd_copy(hp, b, part).wait_recv()
            x = hf[b, part]
            d = 1 + 2 * core
            ss[b, part] = ss[b, part] + ws[d, rows] * x
            ls[b, part] = ls[b, part] + wl[d, rows] * x

        @pl.when((b == 1) & has_right)
        def _():
            side_right(part).start()

        @pl.when((b == 0) & has_left)
        def _():
            side_left(part).start()

        return carry

    lax.fori_loop(0, 2 * UNITS, units, 0)

    def finish(t, carry):
        b = t // UNITS
        part = lax.rem(t, UNITS)

        @pl.when((b == 0) & has_left)
        def _():
            side_right(part).wait_recv()

        @pl.when((b == 1) & has_right)
        def _():
            side_left(part).wait_recv()

        away = jnp.where(jnp.where(b == 0, has_left, has_right), sin[b, part], 0.0)
        rows = pl.ds(pl.multiple_of(lax.rem(t, CUTS) * ROWS, ROWS), ROWS)
        out[0, b, part // CUTS, rows, :] = ls[b, part] + ss[1 - b, part] + away
        return carry

    lax.fori_loop(0, 2 * UNITS, finish, 0)

    @pl.when(has_right)
    def _():
        for part in range(UNITS):
            side_right(part).wait_send()

        @pl.when((s == 1) | (core == 1))
        def _():
            left_copy().wait_send()

    @pl.when(has_left)
    def _():
        for part in range(UNITS):
            side_left(part).wait_send()

        @pl.when((s == 2) | (core == 1))
        def _():
            right_copy().wait_send()

    @pl.when(middle & (core == 0))
    def _():
        far_left_copy().wait_send()
        system_copy(first_block).wait_send()
        system_copy(last_block).wait_send()

    for b in range(2):
        for part in range(UNITS):
            own_copy(b, part).wait_send()

            @pl.when(has_p)
            def _():
                y_copy(True, b, part).wait_send()

            @pl.when(has_m)
            def _():
                y_copy(False, b, part).wait_send()

            @pl.when(((core == 0) & has_p) | ((core == 1) & has_m))
            def _():
                fwd_copy(hp, b, part).wait_send()


def local(onsite, hopping, coupling, broadening, born_sigma, phonon_shift, phonon_local, phonon_side):
    vmem = pl.BlockSpec(memory_space=pltpu.VMEM)
    smem = pl.BlockSpec(memory_space=pltpu.SMEM)
    hbm = pl.BlockSpec(memory_space=pl.ANY)
    dma = pltpu.SemaphoreType.DMA
    block = (2, N, N)
    pieces = (UNITS, ROWS, N)
    return pl.pallas_call(
        kernel,
        out_shape=pltpu.VMEM(born_sigma.shape, F32),
        in_specs=[vmem, hbm, hbm, smem, hbm, smem, hbm, hbm],
        out_specs=vmem,
        scratch_shapes=[
            pltpu.VMEM((2, N, N), F32),
            pltpu.VMEM((2, N, N), F32),
            pltpu.VMEM((2, 2, N, N), F32),
            pltpu.VMEM((MODES, N, N), F32),
            pltpu.VMEM((MODES, N, N), F32),
            dma((8,)),
            pltpu.VMEM((4,) + block, F32),
            pltpu.VMEM((4, 4, N, N), BF16),
            pltpu.VMEM((9,) + block, F32),
            pltpu.VMEM((5,) + pieces, F32),
            pltpu.VMEM((1,) + pieces, F32),
            pltpu.VMEM((2,) + pieces, F32),
            pltpu.VMEM((2,) + pieces, F32),
            pltpu.VMEM((2,) + pieces, F32),
            pltpu.VMEM((2,) + pieces, F32),
            pltpu.VMEM((5, CUTS, ROWS, N), F32),
            pltpu.VMEM((5, CUTS, ROWS, N), F32),
            pltpu.VMEM((2,) + pieces, F32),
            pltpu.VMEM((2,) + pieces, F32),
            pltpu.VMEM((2,) + pieces, F32),
            pltpu.VMEM(block, F32),
            dma((3,)), dma((2,)),
            dma((2, 2, UNITS)), dma((2, 2, UNITS)),
            dma((2, UNITS)), dma((2, UNITS)),
            dma((2, UNITS)), dma((2, UNITS)),
            dma((2, UNITS)), dma((2, UNITS)),
            dma((3,)), dma((3,)),
            pltpu.SemaphoreType.REGULAR,
        ],
        compiler_params=pltpu.CompilerParams(
            collective_id=0, has_side_effects=True, vmem_limit_bytes=56 * 2**20
        ),
        cost_estimate=pl.CostEstimate(flops=6 * 60 * 2 * N**3, bytes_accessed=6 * 2**20, transcendentals=0),
    )(onsite, hopping, coupling, broadening, born_sigma, phonon_shift, phonon_local, phonon_side)


def solution(mesh):
    in_specs = (
        P("section", None),
        P("section", None, None),
        P("section", None, None),
        P("energy"),
        P("energy", "section", None, None, None),
        P(),
        P(),
        P(),
    )
    out_specs = P("energy", "section", None, None, None)
    return jax.shard_map(local, mesh=mesh, in_specs=in_specs, out_specs=out_specs, check_vma=False)
```

```python
import jax
import jax.numpy as jnp
from jax import lax
from jax.experimental import pallas as pl
from jax.experimental.pallas import tpu as pltpu
from jax.sharding import PartitionSpec as P

MODES = 4
N = 256
F32 = jnp.float32
BF16 = jnp.bfloat16
MESH = pl.DeviceIdType.MESH

L, R, G = 4, 8, 12
ORDERS = (
    ((L, L + 1, G + 1, R + 1, G), (L, L + 1, L + 2, L + 3, G + 1, R + 1, G),
     (R + 1, R, R + 3, R + 2, G, L, G + 1), (R + 1, R, G, L, G + 1)),
    ((L, L + 1, G + 1, R + 1, G), (L, L + 1, R + 1, R, G + 1, G),
     (R + 1, R, L, L + 1, G, G + 1), (R + 1, R, G, L, G + 1)),
)
SLOTS = 7
CUTS = 2
UNITS = 2 * CUTS
ROWS = N // CUTS


def order_code(steps):
    return sum(step * 16**i for i, step in enumerate(steps))


def cat(parts, axis):
    return jnp.concatenate(parts, axis=axis)


def split(x):
    hi = x.astype(BF16)
    return hi, (x - hi.astype(F32)).astype(BF16)


def dot3(a, b):
    def dot(x, y):
        return jnp.dot(x, y, preferred_element_type=F32)

    return dot(a[0], b[0]) + dot(a[1], b[0]) + dot(a[0], b[1])


def halves(re, im):
    return split(re), split(im), split(re + im)


def cdot(a, b):
    p1 = dot3(a[0], b[0])
    p2 = dot3(a[1], b[1])
    p3 = dot3(a[2], b[2])
    return p1 - p2, p3 - p1 - p2


def diagonal_mask():
    return lax.broadcasted_iota(jnp.int32, (N, N), 0) == lax.broadcasted_iota(jnp.int32, (N, N), 1)


def inverse(mr, mi):
    eye = diagonal_mask()

    def reciprocal(axis):
        dr = jnp.sum(jnp.where(eye, mr, 0.0), axis=axis, keepdims=True)
        di = jnp.sum(jnp.where(eye, mi, 0.0), axis=axis, keepdims=True)
        modulus = dr * dr + di * di
        return dr / modulus, -di / modulus

    xr, xi = reciprocal(0)
    rr = jnp.where(eye, 0.0, mi * xi - mr * xr)
    ri = jnp.where(eye, 0.0, -(mr * xi + mi * xr))
    r = halves(rr, ri)
    sr, si = cdot(r, r)
    s = halves(sr, si)
    tr, ti = cdot(s, s)
    ur, ui = cdot(r, s)
    yr = jnp.where(eye, 1.0, rr) + sr + ur
    yi = ri + si + ui
    ur, ui = cdot(halves(yr, yi), halves(tr, ti))
    yr = yr + ur
    yi = yi + ui
    cr, ci = reciprocal(1)
    return yr * cr - yi * ci, yr * ci + yi * cr


def couple(a, gr, gi, b):
    gr, gi = split(gr), split(gi)
    g = (cat([gr[0], gi[0]], 1), cat([gr[1], gi[1]], 1))
    hi, lo = split(dot3(a, g))
    hi = cat([hi[:, :N], hi[:, N:]], 0)
    lo = cat([lo[:, :N], lo[:, N:]], 0)
    both = dot3((hi, lo), b)
    return both[:N], both[N:]


def kernel(
    onsite, hop_in, coup_in, broad, born_in, shift, ploc_in, pside_in, out,
    hop, coup, born, ploc, pside, load,
    system, links, sig, green, late, hp, hm, ho, hf, wl, ws, ls, ss, sin, fcoup,
    chain_s, chain_r, y_s, y_r, o_s, o_r, f_s, f_r, side_s, side_r, pre_s, pre_r, go,
):
    e = lax.axis_index("energy")
    s = lax.axis_index("section")
    core = lax.rem(e, 2)
    other = e + 1 - 2 * core
    has_p = e < 30
    has_m = e >= 2
    has_right = s < 3
    has_left = s > 0
    middle = (s == 1) | (s == 2)
    early = jnp.where(s < 2, 1, 0)

    opening = jnp.where(s < 2, 0, 1)

    def loads(b):
        return [
            pltpu.make_async_copy(source.at[b], target.at[b], load.at[3 * b + k])
            for k, (source, target) in enumerate(((hop_in, hop), (born_in.at[0], born), (coup_in, coup)))
        ]

    def phonon_loads():
        return [
            pltpu.make_async_copy(ploc_in, ploc, load.at[6]),
            pltpu.make_async_copy(pside_in, pside, load.at[7]),
        ]

    for b in (opening, 1 - opening):
        for copy in loads(b):
            copy.start()
    for copy in phonon_loads():
        copy.start()

    barrier = pltpu.get_barrier_semaphore()

    def greet(cond, where):
        @pl.when(cond)
        def _():
            pl.semaphore_signal(barrier, inc=1, device_id=where, device_id_type=MESH)

    for distance in (1, 2, 3):
        pl.semaphore_signal(
            barrier, inc=1, device_id={"section": lax.rem(s + distance, 4)}, device_id_type=MESH
        )
    greet(has_p, {"energy": lax.rem(e + 2, 32)})
    greet(has_m, {"energy": lax.rem(e + 30, 32)})
    pl.semaphore_signal(barrier, inc=1, device_id={"energy": other}, device_id_type=MESH)

    def remote(src, dst, ssem, rsem, where):
        return pltpu.make_async_remote_copy(
            src_ref=src, dst_ref=dst, send_sem=ssem, recv_sem=rsem, device_id=where, device_id_type=MESH
        )

    def left_copy():
        return remote(sig.at[5], sig.at[1], chain_s.at[0], chain_r.at[0], {"section": lax.rem(s + 1, 4)})

    def right_copy():
        return remote(green.at[2], late.at[0], chain_s.at[1], chain_r.at[1], {"section": lax.rem(s + 3, 4)})

    def far_left_copy():
        return remote(sig.at[8], sig.at[1], chain_s.at[2], chain_r.at[0], {"section": lax.rem(s + 2, 4)})

    def far_right_copy():
        return remote(green.at[4], late.at[0], chain_s.at[2], chain_r.at[1], {"section": lax.rem(s + 2, 4)})

    swap = {"section": lax.rem(7 - s, 4)}

    def system_copy(b):
        return remote(system.at[b], system.at[2 + b], pre_s.at[b], pre_r.at[b], swap)

    def coupling_copy():
        return remote(coup, fcoup, pre_s.at[2], pre_r.at[2], swap)

    def y_copy(up, b, part):
        if up:
            return remote(green.at[b, part], hm.at[b, part], y_s.at[0, b, part], y_r.at[0, b, part],
                          {"energy": lax.rem(e + 2, 32)})
        return remote(green.at[b, part], hp.at[b, part], y_s.at[1, b, part], y_r.at[1, b, part],
                      {"energy": lax.rem(e + 30, 32)})

    def own_copy(b, part):
        return remote(green.at[b, part], ho.at[b, part], o_s.at[b, part], o_r.at[b, part], {"energy": other})

    def send_block(b):
        for part in range(UNITS):
            @pl.when(has_p)
            def _():
                y_copy(True, b, part).start()

            @pl.when(has_m)
            def _():
                y_copy(False, b, part).start()

    def fwd_copy(src, b, part):
        return remote(src.at[b, part], hf.at[b, part], f_s.at[b, part], f_r.at[b, part], {"energy": other})

    def side_right(part):
        return remote(ss.at[1, part], sin.at[0, part], side_s.at[1, part], side_r.at[0, part],
                      {"section": lax.rem(s + 1, 4)})

    def side_left(part):
        return remote(ss.at[0, part], sin.at[1, part], side_s.at[0, part], side_r.at[1, part],
                      {"section": lax.rem(s + 3, 4)})

    energy = -2.0 + 4.0 * e.astype(F32) / 31.0
    eta = broad[0]

    def link_halves(v, place):
        vh, vl = split(v)
        links[place, 0] = vh
        links[place, 1] = vl
        vh, vl = split(v.T)
        links[place, 2] = vh
        links[place, 3] = vl

    def setup(t, carry):
        b = opening + t - 2 * opening * t
        for copy in loads(b):
            copy.wait()
        eye = diagonal_mask()
        h = hop[b]
        ham = 0.5 * (h + h.T)
        system[b, 0] = jnp.where(eye, energy - onsite[pl.ds(b, 1), :], 0.0) - ham - born[b, 0]
        system[b, 1] = jnp.where(eye, eta, 0.0) - born[b, 1]
        link_halves(coup[b], b)
        return carry

    lax.fori_loop(0, 2, setup, 0)
    sig[0] = jnp.zeros((2, N, N), F32)

    @pl.when(s == 0)
    def _():
        sig[1] = jnp.zeros((2, N, N), F32)

    @pl.when(s == 3)
    def _():
        sig[4] = jnp.zeros((2, N, N), F32)

    def everyone_is_in():
        pl.semaphore_wait(barrier, 4 + has_p.astype(jnp.int32) + has_m.astype(jnp.int32))

    def weights():
        for copy in phonon_loads():
            copy.wait()

        def one(d, carry):
            wloc = jnp.zeros((N, N), F32)
            wside = jnp.zeros((N, N), F32)
            for k in range(MODES):
                on = jnp.where(shift[k] == d - 2, 1.0, 0.0)
                wloc = wloc + on * ploc[k]
                wside = wside + on * pside[k]
            wl[d] = wloc.reshape(CUTS, ROWS, N)
            ws[d] = wside.reshape(CUTS, ROWS, N)
            return carry

        lax.fori_loop(0, 5, one, 0)

    first_block = lax.rem(s, 2)
    last_block = 1 - first_block

    @pl.when(middle)
    def _():
        everyone_is_in()

    @pl.when(middle & (core == 0))
    def _():
        coupling_copy().start()
        system_copy(first_block).start()

    @pl.when(middle)
    def _():
        weights()

    @pl.when(middle & (core == 0))
    def _():
        coupling_copy().wait_recv()

        def foreign(b, carry):
            link_halves(fcoup[b], 2 + b)
            return carry

        lax.fori_loop(0, 2, foreign, 0)
        coupling_copy().wait_send()
        system_copy(last_block).start()

    def pick(b, values):
        return jnp.where(b == 0, values[0], jnp.where(b == 1, values[1], jnp.where(b == 2, values[2], values[3])))

    def slot(i, code):
        digit = lax.rem(code, 16)
        kind = digit // 4
        b = lax.rem(digit, 4)
        is_l = kind == 1
        is_r = kind == 2

        @pl.when((i == 2) & jnp.logical_not(middle))
        def _():
            weights()

        @pl.when(i == pick(s, (9, 0, 4 - 2 * core, 2)))
        def _():
            left_copy().wait_recv()

        @pl.when(i == pick(s, (2, 4 - 2 * core, 0, 9)))
        def _():
            right_copy().wait_recv()
            re, im = couple((links[1, 0], links[1, 1]), late[0, :CUTS].reshape(N, N), late[0, CUTS:].reshape(N, N), (links[1, 2], links[1, 3]))
            sig[4, 0] = re
            sig[4, 1] = im

        @pl.when(kind > 0)
        def _():
            @pl.when(b >= 2)
            def _():
                system_copy(b - 2).wait_recv()

            first = jnp.where(is_r, 0, pick(b, (1, 2, 5, 7)))
            second = jnp.where(is_l, 0, pick(b, (3, 4, 8, 7)))
            place = jnp.where(kind == 3, b, jnp.where(is_r, pick(b, (2, 3, 4, 3)), 3))
            re, im = inverse(
                system[b, 0] - sig[first, 0] - sig[second, 0], system[b, 1] - sig[first, 1] - sig[second, 1]
            )
            green[place, :CUTS] = re.reshape(CUTS, ROWS, N)
            green[place, CUTS:] = im.reshape(CUTS, ROWS, N)

            at_end = (i == 1) & jnp.logical_not(middle)

            @pl.when(at_end)
            def _():
                everyone_is_in()

            @pl.when(at_end & (s == 3) & (core == 1))
            def _():
                pl.semaphore_wait(go, 1)

            @pl.when(is_r & (b == 0))
            def _():
                right_copy().start()

            @pl.when(is_r & (b == 2))
            def _():
                far_right_copy().start()

            @pl.when(is_l | (is_r & ((b == 1) | (b == 3) | ((b == 0) & (s == 2) & (core == 0)))))
            def _():
                v = jnp.where(is_l, b, pick(b, (3, 0, 0, 2)))
                a0 = jnp.where(is_l, 2, 0)
                b0 = 2 - a0
                target = jnp.where(is_l, pick(b, (2, 5, 7, 8)), pick(b, (7, 3, 0, 8)))
                re, im = couple((links[v, a0], links[v, a0 + 1]), green[place, :CUTS].reshape(N, N), green[place, CUTS:].reshape(N, N),
                                (links[v, b0], links[v, b0 + 1]))
                sig[target, 0] = re
                sig[target, 1] = im

            @pl.when(at_end & (s == 0) & (core == 1))
            def _():
                pl.semaphore_wait(go, 1)

            @pl.when(is_l & (b == 1))
            def _():
                left_copy().start()

            @pl.when(is_l & (b == 3))
            def _():
                far_left_copy().start()

            @pl.when(at_end & (core == 0))
            def _():
                @pl.when(s == 0)
                def _():
                    left_copy().wait_send()

                @pl.when(s == 3)
                def _():
                    right_copy().wait_send()

                pl.semaphore_signal(go, inc=1, device_id={"energy": other}, device_id_type=MESH)

            @pl.when(kind == 3)
            def _():
                for part in range(UNITS):
                    own_copy(b, part).start()

                @pl.when(b == early)
                def _():
                    send_block(b)

        return code // 16

    codes = [pick(s, [order_code(x) for x in orders]) for orders in ORDERS]
    lax.fori_loop(0, SLOTS, slot, jnp.where(core == 0, codes[0], codes[1]))

    def units(t, carry):
        half = t // UNITS
        b = early + half - 2 * early * half
        part = lax.rem(t, UNITS)
        rows = lax.rem(t, CUTS)

        @pl.when(t == 0)
        def _():
            send_block(1 - early)

        @pl.when(has_p)
        def _():
            y_copy(False, b, part).wait_recv()

            @pl.when(core == 0)
            def _():
                fwd_copy(hp, b, part).start()

        @pl.when(has_m)
        def _():
            y_copy(True, b, part).wait_recv()

            @pl.when(core == 1)
            def _():
                fwd_copy(hm, b, part).start()

        own_copy(b, part).wait_recv()
        x = green[b, part]
        near = ho[b, part]
        up = jnp.where(has_p, hp[b, part], 0.0)
        down = jnp.where(has_m, hm[b, part], 0.0)
        d = 3 - 2 * core
        ls[b, part] = wl[2, rows] * x + wl[d, rows] * near + wl[4, rows] * up + wl[0, rows] * down
        ss[b, part] = ws[2, rows] * x + ws[d, rows] * near + ws[4, rows] * up + ws[0, rows] * down

        @pl.when(((core == 0) & has_m) | ((core == 1) & has_p))
        def _():
            fwd_copy(hp, b, part).wait_recv()
            x = hf[b, part]
            d = 1 + 2 * core
            ss[b, part] = ss[b, part] + ws[d, rows] * x
            ls[b, part] = ls[b, part] + wl[d, rows] * x

        @pl.when((b == 1) & has_right)
        def _():
            side_right(part).start()

        @pl.when((b == 0) & has_left)
        def _():
            side_left(part).start()

        return carry

    lax.fori_loop(0, 2 * UNITS, units, 0)

    def finish(t, carry):
        b = t // UNITS
        part = lax.rem(t, UNITS)

        @pl.when((b == 0) & has_left)
        def _():
            side_right(part).wait_recv()

        @pl.when((b == 1) & has_right)
        def _():
            side_left(part).wait_recv()

        away = jnp.where(jnp.where(b == 0, has_left, has_right), sin[b, part], 0.0)
        rows = pl.ds(pl.multiple_of(lax.rem(t, CUTS) * ROWS, ROWS), ROWS)
        out[0, b, part // CUTS, rows, :] = ls[b, part] + ss[1 - b, part] + away
        return carry

    lax.fori_loop(0, 2 * UNITS, finish, 0)

    @pl.when(has_right)
    def _():
        for part in range(UNITS):
            side_right(part).wait_send()

        @pl.when((s == 1) | (core == 1))
        def _():
            left_copy().wait_send()

    @pl.when(has_left)
    def _():
        for part in range(UNITS):
            side_left(part).wait_send()

        @pl.when((s == 2) | (core == 1))
        def _():
            right_copy().wait_send()

    @pl.when(middle & (core == 0))
    def _():
        far_left_copy().wait_send()
        system_copy(first_block).wait_send()
        system_copy(last_block).wait_send()

    for b in range(2):
        for part in range(UNITS):
            own_copy(b, part).wait_send()

            @pl.when(has_p)
            def _():
                y_copy(True, b, part).wait_send()

            @pl.when(has_m)
            def _():
                y_copy(False, b, part).wait_send()

            @pl.when(((core == 0) & has_p) | ((core == 1) & has_m))
            def _():
                fwd_copy(hp, b, part).wait_send()


def local(onsite, hopping, coupling, broadening, born_sigma, phonon_shift, phonon_local, phonon_side):
    vmem = pl.BlockSpec(memory_space=pltpu.VMEM)
    smem = pl.BlockSpec(memory_space=pltpu.SMEM)
    hbm = pl.BlockSpec(memory_space=pl.ANY)
    dma = pltpu.SemaphoreType.DMA
    block = (2, N, N)
    pieces = (UNITS, ROWS, N)
    return pl.pallas_call(
        kernel,
        out_shape=pltpu.VMEM(born_sigma.shape, F32),
        in_specs=[vmem, hbm, hbm, smem, hbm, smem, hbm, hbm],
        out_specs=vmem,
        scratch_shapes=[
            pltpu.VMEM((2, N, N), F32),
            pltpu.VMEM((2, N, N), F32),
            pltpu.VMEM((2, 2, N, N), F32),
            pltpu.VMEM((MODES, N, N), F32),
            pltpu.VMEM((MODES, N, N), F32),
            dma((8,)),
            pltpu.VMEM((4,) + block, F32),
            pltpu.VMEM((4, 4, N, N), BF16),
            pltpu.VMEM((9,) + block, F32),
            pltpu.VMEM((5,) + pieces, F32),
            pltpu.VMEM((1,) + pieces, F32),
            pltpu.VMEM((2,) + pieces, F32),
            pltpu.VMEM((2,) + pieces, F32),
            pltpu.VMEM((2,) + pieces, F32),
            pltpu.VMEM((2,) + pieces, F32),
            pltpu.VMEM((5, CUTS, ROWS, N), F32),
            pltpu.VMEM((5, CUTS, ROWS, N), F32),
            pltpu.VMEM((2,) + pieces, F32),
            pltpu.VMEM((2,) + pieces, F32),
            pltpu.VMEM((2,) + pieces, F32),
            pltpu.VMEM(block, F32),
            dma((3,)), dma((2,)),
            dma((2, 2, UNITS)), dma((2, 2, UNITS)),
            dma((2, UNITS)), dma((2, UNITS)),
            dma((2, UNITS)), dma((2, UNITS)),
            dma((2, UNITS)), dma((2, UNITS)),
            dma((3,)), dma((3,)),
            pltpu.SemaphoreType.REGULAR,
        ],
        compiler_params=pltpu.CompilerParams(
            collective_id=0, has_side_effects=True, vmem_limit_bytes=56 * 2**20
        ),
        cost_estimate=pl.CostEstimate(flops=6 * 60 * 2 * N**3, bytes_accessed=6 * 2**20, transcendentals=0),
    )(onsite, hopping, coupling, broadening, born_sigma, phonon_shift, phonon_local, phonon_side)


def solution(mesh):
    in_specs = (
        P("section", None),
        P("section", None, None),
        P("section", None, None),
        P("energy"),
        P("energy", "section", None, None, None),
        P(),
        P(),
        P(),
    )
    out_specs = P("energy", "section", None, None, None)
    return jax.shard_map(local, mesh=mesh, in_specs=in_specs, out_specs=out_specs, check_vma=False)
```
